128 devices in a mesh: pts: 16 (over y_hi, x, core), coef: 8 (over z, y_lo).
Axes of the slice: x: 4, y: 4 (y_hi: 2, y_lo: 2; y = y_hi * 2 + y_lo), z: 4, core: 2. Of those that a mesh axis runs over, the one named last changes fastest.
Arguments:
- colatitude: float32 [4096], P('pts'), may hold values from 0.96 to 2.18
- longitude: float32 [1310720], P('pts'), may hold values from -3.140625 to 3.140625
- tile_of_point: int32 [1310720], P('pts'), may hold values from 0 to 4095, as said below
- order_of_slot: int32 [320], P('coef'), may hold values from 0 to 319, each once
- observations: float32 [1310720], P('pts'), may hold values from -6 to 6
- obs_weight: float32 [1310720], P('pts'), may hold values from 0.2 to 5
- prior: float32 [301], replicated, may hold values from 1 to 10
Outputs:
- coefficients: float32 [301, 2, 320], P(None, None, 'coef')
- point_residual: float32 [1310720], P('pts')
The draws below stay inside these ranges and needn't reach their ends.
Inputs may be any that keep to these rules, and one draw needn't show every extreme that they name: `tile_of_point`: the k-th block of 81920 points lies in tiles k * 256 to (k + 1) * 256 - 1. `order_of_slot`: each number once; slots holding a number above 300 are empty and contribute nothing.
All inputs are finite; a program needn't handle non-finite values.
Results may differ from the reference program's by a relative error of at most 0.0003.
Values sent between devices are 32-bit elements; how exact they have to be, the bound alone decides.
No kernel may reach another device: no remote copies, remote signals or barrier semaphores. Data moves between devices by JAX's collectives and lax.ppermute only.
A program may use at most 64 MiB of HBM per device.

```python
import math
import jax
import jax.numpy as jnp
from jax import lax

DEGREES = 301
ORD_SLOTS = 320
ITERS = 2
PTS_DEV = 81920
TILE_DEV = 256
POINTS = 1310720
TILES = 4096


def draw_tile_of_point(key, part):
    key = jax.random.fold_in(key, 5)
    groups = TILES // TILE_DEV
    local_ids = jax.random.randint(key, (groups, PTS_DEV), 0, TILE_DEV)
    local_ids = local_ids.at[:, 0].set(0).at[:, 1].set(TILE_DEV - 1)
    offsets = jnp.arange(groups, dtype=jnp.int32)[:, None] * TILE_DEV
    return (local_ids + offsets).reshape(-1).astype(jnp.int32)


def steps_of(own_key, extent, shards, smallest, top_value):
    factor_of = 1.0
    for position, blocks in shards:
        heights = jax.random.uniform(jax.random.fold_in(jax.random.fold_in(own_key, 6), position), (blocks,), jnp.float32, smallest / len(shards), top_value / len(shards))
        factor_of = factor_of * jnp.repeat(jnp.exp(heights), extent[position] // blocks).reshape((-1,) + (1,) * (len(extent) - 1 - position))
    return factor_of


def centred(rng, extent, deviation, bound, split=(), held_as=jnp.bfloat16):
    gain = steps_of(rng, extent, split, -0.22, 0.18) if split else 1.0
    entries = jax.random.normal(rng, extent, jnp.float32) * deviation * gain
    return jnp.minimum(jnp.maximum(entries, -bound), bound).astype(held_as)


def setup_inputs(seed: int = 0) -> dict:
    key_of = jax.random.split(jax.random.key(seed), 8)
    return {
        "colatitude": jnp.clip(0.96 + 1.22 * jax.random.uniform(key_of[0], (TILES,), jnp.float32) ** steps_of(key_of[0], (TILES,), ((0, 16),), -0.2, 0.2), 0.96, 2.18),
        "longitude": jnp.clip(jax.random.uniform(key_of[1], (POINTS,), jnp.float32, -3.140625, 3.140625), -3.140625, 3.140625),
        "tile_of_point": draw_tile_of_point(jax.random.fold_in(key_of[7], 71), 0),
        "order_of_slot": jax.random.permutation(key_of[3], ORD_SLOTS).astype(jnp.int32),
        "observations": centred(key_of[4], (POINTS,), 1.0, 6.0, ((0, 16),), jnp.float32),
        "obs_weight": jnp.clip(jnp.exp(math.log(5.0) - 3.218876 * jax.random.uniform(key_of[5], (POINTS,), jnp.float32) ** steps_of(key_of[5], (POINTS,), ((0, 16),), -0.2, 0.2)), 0.2, 5.0),
        "prior": jnp.clip(jnp.exp(jax.random.uniform(key_of[6], (DEGREES,), jnp.float32, math.log(1.0), math.log(10.0))), 1.0, 10.0),
    }


def degree_factors(degree, orders):
    plus_sum = degree + orders
    minus_sum = degree - orders
    upward = jnp.sqrt(jnp.maximum((2.0 * degree - 1.0) * (2.0 * degree + 1.0), 0.0) / jnp.maximum(minus_sum * plus_sum, 1.0))
    backward = jnp.sqrt((2.0 * degree + 1.0) * jnp.maximum(plus_sum - 1.0, 0.0) * jnp.maximum(minus_sum - 1.0, 0.0) / jnp.maximum((2.0 * degree - 3.0) * minus_sum * plus_sum, 1.0))
    return (upward, backward)

def next_row(degree, orders, cosine, sectoral, recent, earlier):
    upward, backward = degree_factors(degree, orders)
    grown = upward * cosine * recent - backward * earlier
    return jnp.where(degree < orders, 0.0, jnp.where(degree == orders, sectoral, grown))

def sectoral_values(orders, sines):
    single = (orders == 0.0).astype(jnp.float32)
    log_lead = 0.5 * (jnp.log(2.0 - single) + lax.lgamma(orders + 1.5) - lax.lgamma(orders * 0.0 + 1.5) - lax.lgamma(orders + 1.0))
    return jnp.exp(log_lead + orders * jnp.log(sines))

def legendre_fold(coeff, orders, cosine, sectoral):
    empty = jnp.zeros(sectoral.shape, jnp.float32)

    def advance(carried, packed):
        recent, earlier, running = carried
        degree, coeff_row = packed
        legendre = next_row(degree, orders, cosine, sectoral, recent, earlier)
        return ((legendre, recent, running + legendre[None] * coeff_row[:, :, None]), None)
    degrees = jnp.arange(DEGREES).astype(jnp.float32)
    initial = (empty, empty, jnp.zeros((2,) + sectoral.shape, jnp.float32))
    return lax.scan(advance, initial, (degrees, coeff))[0][2]

def legendre_unfold(folded, orders, cosine, sectoral):
    empty = jnp.zeros(sectoral.shape, jnp.float32)

    def advance(carried, degree):
        recent, earlier = carried
        legendre = next_row(degree, orders, cosine, sectoral, recent, earlier)
        return ((legendre, recent), lax.optimization_barrier(jnp.sum(legendre[None] * folded, axis=2)))
    degrees = jnp.arange(DEGREES).astype(jnp.float32)
    return lax.scan(advance, (empty, empty), degrees)[1]

def point_values(fourier, orders_flat, longitude, tile_of_point):

    def one_block(packed):
        angles, tile_ids = packed
        picked = jnp.take(fourier, tile_ids, axis=2)
        phases = orders_flat[:, None] * angles[None, :]
        return lax.optimization_barrier(jnp.sum(jnp.cos(phases) * picked[0] + jnp.sin(phases) * picked[1], axis=0))
    blocks = (longitude.reshape(-1, PTS_DEV), tile_of_point.reshape(-1, PTS_DEV))
    return lax.map(one_block, blocks).reshape(-1)

def point_fold(point_field, orders_flat, longitude, tile_of_point):
    slot_count = orders_flat.shape[0]

    def one_block(running, packed):
        angles, tile_ids, field_block = packed
        phases = orders_flat[:, None] * angles[None, :]
        stacked = jnp.concatenate([jnp.cos(phases) * field_block[None, :], jnp.sin(phases) * field_block[None, :]], 0)
        return (running + jax.ops.segment_sum(stacked.T, tile_ids, TILES).T, None)
    initial = jnp.zeros((2 * slot_count, TILES), jnp.float32)
    blocks = (longitude.reshape(-1, PTS_DEV), tile_of_point.reshape(-1, PTS_DEV), point_field.reshape(-1, PTS_DEV))
    folded = lax.scan(one_block, initial, blocks)[0]
    return folded.reshape(2, slot_count, TILES)

def reference(colatitude, longitude, tile_of_point, order_of_slot, observations, obs_weight, prior):
    orders_flat = order_of_slot.astype(jnp.float32)
    orders = orders_flat[:, None]
    cosine = jnp.cos(colatitude)[None, :]
    sectoral = sectoral_values(orders, jnp.sin(colatitude)[None, :])
    inverse_degree = 1.0 / DEGREES

    def synthesize(vector):
        fourier = legendre_fold(vector, orders, cosine, sectoral)
        return point_values(fourier, orders_flat, longitude, tile_of_point) * inverse_degree

    def project(point_field):
        folded = point_fold(obs_weight * point_field, orders_flat, longitude, tile_of_point)
        return legendre_unfold(folded, orders, cosine, sectoral) * inverse_degree

    def normal(vector):
        return project(synthesize(vector)) + prior[:, None, None] * vector
    rhs = project(observations)
    solution = jnp.zeros_like(rhs)
    residual = rhs
    direction = rhs
    norm_now = jnp.sum(residual * residual)
    for iteration in range(ITERS):
        applied = normal(direction)
        step_size = norm_now / jnp.sum(direction * applied)
        solution = solution + step_size * direction
        residual = residual - step_size * applied
        norm_next = jnp.sum(residual * residual)
        direction = residual + norm_next / norm_now * direction
        norm_now = norm_next
    return (solution, observations - synthesize(solution))
```

```python
import math
import numpy as np
import jax
import jax.numpy as jnp
from jax import lax
from jax.experimental import pallas as pl
from jax.experimental.pallas import tpu as pltpu
from jax.sharding import PartitionSpec as P

DEGREES = 301
DEG_PAD = 304
SLOTS = 40
TILES = 256
GROUPS = 8
OWN_TILES = TILES // GROUPS
ORDERS = 320
GRID = 1280
HALF = GRID // 2
LANES = 128
INV = 1.0 / DEGREES
BF = jnp.bfloat16
F32 = jnp.float32
ROUNDER = 12582912.0

NN = (((1,), (0,)), ((), ()))
NT = (((1,), (1,)), ((), ()))


def fit_even(f, terms):
    r = 0.502 * np.cos((np.arange(400) + 0.5) * np.pi / 800)
    a = np.stack([r ** (2 * k) for k in range(terms)], 1)
    return [float(v) for v in np.linalg.lstsq(a, f(r), rcond=None)[0]]


SIN_TERMS = fit_even(lambda r: np.sin(np.pi * r) / r, 5)
COS_TERMS = fit_even(lambda r: np.cos(np.pi * r), 5)


def horner(x, terms):
    total = terms[-1] * x + terms[-2]
    for term in terms[-3::-1]:
        total = total * x + term
    return total


def turn_trig(order, high, low):
    whole = order * high
    near = (whole + ROUNDER) - ROUNDER
    part = (whole - near) + order * low
    square = part * part
    s = horner(square, SIN_TERMS) * part
    c = horner(square, COS_TERMS)
    twice = s + s
    return 1.0 - twice * s, twice * c


def split(x):
    high = x.astype(BF)
    return high, (x - high.astype(F32)).astype(BF)


def dot(a, b, dims):
    return lax.dot_general(a, b, dims, preferred_element_type=F32)


def mm3(x, b_high, b_low, dims):
    rows = x.shape[0]
    high, low = split(x)
    both = dot(jnp.concatenate([high, low], 0), b_high, dims)
    return both[:rows] + both[rows:] + dot(high, b_low, dims)


def vmem(n):
    return [pl.BlockSpec(memory_space=pltpu.VMEM)] * n


SMEM = pl.BlockSpec(memory_space=pltpu.SMEM)


def params(mib):
    return pltpu.CompilerParams(vmem_limit_bytes=mib * 2**20)


def cost(flops, bytes_accessed):
    return pl.CostEstimate(flops=flops, bytes_accessed=bytes_accessed, transcendentals=0)


def tile_hits(tile_row, width):
    ids = lax.broadcasted_iota(jnp.int32, (TILES, width), 0).astype(F32).astype(BF)
    return jnp.where(ids == tile_row.astype(BF), jnp.ones((), BF), jnp.zeros((), BF))


WIDTH = 512
PER_STEP = 2


def moments_kernel(points, orders, field, w_first, w_second, total):
    total[...] = jnp.zeros_like(total)
    order = jnp.broadcast_to(orders[:, 0:1], (SLOTS, WIDTH))

    def step(i, carry):
        add = None
        for part in range(PER_STEP):
            data = points[:, pl.ds(pl.multiple_of((i * PER_STEP + part) * WIDTH, WIDTH), WIDTH)]
            high, low, weight, value = data[0:1], data[1:2], data[2:3], data[3:4]
            c_far, s_far = data[4:5], data[5:6]
            c, s = turn_trig(order, high, low)
            wc, ws = weight * c, weight * s
            rows = jnp.concatenate(
                [value * c, value * s, wc, ws, wc * c_far - ws * s_far, ws * c_far + wc * s_far], 0
            )
            rows_high, rows_low = split(rows)
            hits = tile_hits(data[6:7], WIDTH)
            got = dot(jnp.concatenate([rows_high, rows_low], 0), hits, NT)
            add = got if add is None else add + got
        total[...] += add
        return carry

    lax.fori_loop(0, points.shape[1] // (WIDTH * PER_STEP), step, 0)
    whole = total[0 : 6 * SLOTS] + total[6 * SLOTS : 12 * SLOTS]
    field[...] = whole[0 : 2 * SLOTS]
    blank = jnp.zeros((LANES - 2 * SLOTS, TILES), F32)
    w_first[...] = jnp.concatenate([whole[2 * SLOTS : 4 * SLOTS], blank], 0).T
    w_second[...] = jnp.concatenate([whole[4 * SLOTS : 6 * SLOTS], blank], 0).T


def moments(points, orders):
    n = points.shape[1]
    return pl.pallas_call(
        moments_kernel,
        out_shape=[
            jax.ShapeDtypeStruct((2 * SLOTS, TILES), F32),
            jax.ShapeDtypeStruct((TILES, LANES), F32),
            jax.ShapeDtypeStruct((TILES, LANES), F32),
        ],
        in_specs=vmem(2),
        out_specs=vmem(3),
        scratch_shapes=[pltpu.VMEM((12 * SLOTS, TILES), F32)],
        compiler_params=params(40),
        cost_estimate=cost(2 * 12 * SLOTS * TILES * n, 32 * n),
    )(points, orders)


def table_kernel(orders, cosine, sectoral, scale, p_high, p_low, left, right):
    order = jnp.broadcast_to(orders[:, 0:1], (SLOTS, TILES))
    order_sq = orders[...] * orders[...]
    cos_row = jnp.broadcast_to(cosine[...], (SLOTS, TILES))
    start = sectoral[...]

    def put(n, value):
        for b in range(SLOTS // 8):
            at = pl.ds(b * 8 * DEG_PAD + n, 8, stride=DEG_PAD)
            left[at, :] = value[8 * b : 8 * b + 8, 0:LANES]
            right[at, :] = value[8 * b : 8 * b + 8, LANES:TILES]

    def step(n, carried):
        recent, earlier, back = carried
        degree = n.astype(F32)
        ratio = jnp.maximum((degree * degree - order_sq) * scale[n], 1e-20)
        up = lax.rsqrt(ratio)
        this_back = ratio * up
        up2 = jnp.concatenate([up, up], 1)
        back2 = jnp.concatenate([back, back], 1)
        grown = up2 * (cos_row * recent - back2 * earlier)
        value = jnp.where(order > degree, 0.0, jnp.where(order == degree, start, grown))
        put(n, value)
        return value, recent, this_back

    empty = jnp.zeros((SLOTS, TILES), F32)
    unset = start * 0.0
    lax.fori_loop(0, DEGREES, step, (unset, unset, order_sq * 0.0))
    for n in range(DEGREES, DEG_PAD):
        put(n, empty)

    def pack(slot, carry):
        at = pl.ds(pl.multiple_of(slot * DEG_PAD, 8), DEG_PAD)
        high, low = split(jnp.concatenate([left[at, :], right[at, :]], 1))
        p_high[slot] = high
        p_low[slot] = low
        return carry

    lax.fori_loop(0, SLOTS, pack, 0)


def legendre_table(orders, cosine, sectoral, scale):
    shape = jax.ShapeDtypeStruct((SLOTS, DEG_PAD, TILES), BF)
    return pl.pallas_call(
        table_kernel,
        out_shape=[shape, shape],
        in_specs=vmem(3) + [SMEM],
        out_specs=vmem(2),
        scratch_shapes=[pltpu.VMEM((SLOTS * DEG_PAD, LANES), F32)] * 2,
        compiler_params=params(48),
        cost_estimate=cost(20 * SLOTS * DEG_PAD * TILES, 4 * SLOTS * DEG_PAD * TILES),
    )(orders, cosine, sectoral, scale)


def by_slot(vector, p_high, p_low, width, dims, put):
    row = lax.broadcasted_iota(jnp.int32, (16, width), 0)

    def group(g, carry):
        at = pl.multiple_of(g * 8, 8)
        rows = jnp.concatenate([vector[pl.ds(at, 8), :], vector[pl.ds(at + SLOTS, 8), :]], 0)
        high, low = split(rows)
        both = jnp.concatenate([high, low], 0)
        out = jnp.zeros((16, width), F32)
        for i in range(8):
            first = dot(both, p_high[at + i], dims)
            total = first[0:16] + first[16:32] + dot(high, p_low[at + i], dims)
            out = jnp.where((row == i) | (row == i + 8), total, out)
        put(at, out)
        return carry

    lax.fori_loop(0, SLOTS // 8, group, 0)


def fold_kernel(vector, p_high, p_low, out, rows):
    def put(at, value):
        rows[pl.ds(at, 8), :] = value[0:8]
        rows[pl.ds(at + SLOTS, 8), :] = value[8:16]

    rows[2 * SLOTS :, :] = jnp.zeros((LANES - 2 * SLOTS, TILES), F32)
    by_slot(vector, p_high, p_low, TILES, NN, put)
    out[...] = rows[...].T


def fold(vector, p_high, p_low):
    return pl.pallas_call(
        fold_kernel,
        out_shape=jax.ShapeDtypeStruct((TILES, LANES), F32),
        in_specs=vmem(3),
        out_specs=pl.BlockSpec(memory_space=pltpu.VMEM),
        scratch_shapes=[pltpu.VMEM((LANES, TILES), F32)],
        compiler_params=params(32),
        cost_estimate=cost(64 * SLOTS * DEG_PAD * TILES, 4 * SLOTS * DEG_PAD * TILES),
    )(vector, p_high, p_low)


def unfold_kernel(flip, field, p_high, p_low, out, rows):
    factor = INV * INV if flip else INV
    if flip:
        rows[...] = field[...].T
        source = rows
    else:
        source = field

    def put(at, value):
        out[pl.ds(at, 8), :] = value[0:8] * factor
        out[pl.ds(at + SLOTS, 8), :] = value[8:16] * factor

    by_slot(source, p_high, p_low, DEG_PAD, NT, put)


def unfold(field, p_high, p_low, flip):
    return pl.pallas_call(
        lambda *refs: unfold_kernel(flip, *refs),
        out_shape=jax.ShapeDtypeStruct((2 * SLOTS, DEG_PAD), F32),
        in_specs=vmem(3),
        out_specs=pl.BlockSpec(memory_space=pltpu.VMEM),
        scratch_shapes=[pltpu.VMEM((LANES, TILES), F32)],
        compiler_params=params(32),
        cost_estimate=cost(64 * SLOTS * DEG_PAD * TILES, 4 * SLOTS * DEG_PAD * TILES),
    )(field, p_high, p_low)


F_ROWS = TILES
EXTRA_FIRST = TILES + 2 * OWN_TILES


def slot_hits(order_row):
    wanted = lax.broadcasted_iota(jnp.int32, (ORDERS, LANES), 0).astype(F32)
    return jnp.where(wanted == order_row, 1.0, 0.0).astype(BF)


def two_halves(x):
    lane = lax.broadcasted_iota(jnp.int32, x.shape, 1)
    return jnp.where(lane < SLOTS, x, 0.0), jnp.where((lane >= SLOTS) & (lane < 2 * SLOTS), x, 0.0)


def to_natural(pieces, hits):
    total = None
    for per_source, hit in zip(pieces, hits):
        rows = [half for x in per_source for half in two_halves(x)]
        high, low = split(jnp.concatenate(rows, 0))
        got = dot(jnp.concatenate([high, low], 0), hit, NT)
        total = got if total is None else total + got
    n = total.shape[0] // 2
    return total[:n] + total[n:]


def grid_first_kernel(me, got, c1, c1l, c2, c2l, s1, s1l, s2, s2l, back, kept):
    mine = pl.multiple_of(me[0] * OWN_TILES, OWN_TILES)
    t = OWN_TILES
    hits = [slot_hits(got[g, EXTRA_FIRST : EXTRA_FIRST + 1, :]) for g in range(GROUPS)]
    nat = to_natural(
        [
            [got[g, pl.ds(mine, t), :], got[g, TILES : TILES + t, :], got[g, TILES + t : TILES + 2 * t, :]]
            for g in range(GROUPS)
        ],
        hits,
    )
    k = lax.broadcasted_iota(jnp.int32, (1, ORDERS), 1)
    k_first = jnp.where(k == 0, 1.0 / GRID, 2.0 / GRID)
    k_second = jnp.where(k + ORDERS <= 2 * (DEGREES - 1), 2.0 / GRID, 0.0)
    even = mm3(jnp.concatenate([nat[0:t], nat[2 * t : 3 * t] * k_first], 0), c1[...], c1l[...], NN)
    odd = mm3(jnp.concatenate([nat[t : 2 * t], nat[3 * t : 4 * t] * k_first], 0), s1[...], s1l[...], NN)
    w_even = even[t:] + mm3(nat[4 * t : 5 * t] * k_second, c2[...], c2l[...], NN)
    w_odd = odd[t:] + mm3(nat[5 * t : 6 * t] * k_second, s2[...], s2l[...], NN)
    even, odd = even[:t], odd[:t]
    h_even = 2.0 * (w_even * even + w_odd * odd)
    h_odd = 2.0 * (w_even * odd + w_odd * even)
    energy = jnp.sum(jnp.sum(h_even * even + h_odd * odd, axis=1, keepdims=True), axis=0, keepdims=True)
    kept[0] = even
    kept[1] = odd
    kept[2] = w_even
    kept[3] = w_odd
    hc = mm3(h_even, c1[...], c1l[...], NT)
    hs = mm3(h_odd, s1[...], s1l[...], NT)
    c_high, c_low = split(hc)
    s_high, s_low = split(hs)
    stack = jnp.concatenate([c_high, c_low, s_high, s_low], 0)
    lane = lax.broadcasted_iota(jnp.int32, (t, LANES), 1)
    for g in range(GROUPS):
        slots = dot(stack, hits[g], NN)
        back[g, 0:t, :] = jnp.where(
            lane < SLOTS, slots[0:t] + slots[t : 2 * t], slots[2 * t : 3 * t] + slots[3 * t :]
        )
        back[g, t : t + 8, :] = jnp.broadcast_to(energy, (8, LANES))


def grid_first(me, got, waves):
    return pl.pallas_call(
        grid_first_kernel,
        out_shape=[
            jax.ShapeDtypeStruct((GROUPS, OWN_TILES + 8, LANES), F32),
            jax.ShapeDtypeStruct((4, OWN_TILES, HALF), F32),
        ],
        in_specs=[SMEM] + vmem(9),
        out_specs=vmem(2),
        compiler_params=params(32),
        cost_estimate=cost(10**9, 5 * 10**6),
    )(me, got, *waves)


def grid_second_kernel(me, ratio, got, kept, c1, c1l, s1, s1l, out):
    mine = pl.multiple_of(me[0] * OWN_TILES, OWN_TILES)
    t = OWN_TILES
    hits = [slot_hits(got[g, TILES : TILES + 1, :]) for g in range(GROUPS)]
    nat = to_natural([[got[g, pl.ds(mine, t), :]] for g in range(GROUPS)], hits)
    even = mm3(nat[0:t], c1[...], c1l[...], NN) + ratio[0] * kept[0]
    odd = mm3(nat[t:], s1[...], s1l[...], NN) + ratio[0] * kept[1]
    w_even, w_odd = kept[2], kept[3]
    terms = 2.0 * w_even * (even * even + odd * odd) + 4.0 * w_odd * (even * odd)
    energy = jnp.sum(jnp.sum(terms, axis=1, keepdims=True), axis=0, keepdims=True)
    out[...] = jnp.broadcast_to(energy, (8, LANES))


def grid_second(me, ratio, got, kept, waves):
    return pl.pallas_call(
        grid_second_kernel,
        out_shape=jax.ShapeDtypeStruct((8, LANES), F32),
        in_specs=[SMEM, SMEM] + vmem(6),
        out_specs=pl.BlockSpec(memory_space=pltpu.VMEM),
        compiler_params=params(32),
        cost_estimate=cost(10**9, 5 * 10**6),
    )(me, ratio, got, kept, *waves)


S_WIDTH = 512


def values_kernel(extra_row, me, points, got, out, z_high, z_low, picked):
    hits = jnp.concatenate(
        [slot_hits(got[g, extra_row : extra_row + 1, :]) for g in range(GROUPS)], 1
    )
    halves = [two_halves(got[g, 0:TILES, :]) for g in range(GROUPS)]
    for c in range(2):
        high, low = split(jnp.concatenate([h[c] for h in halves], 1))
        z_high[pl.ds(c * ORDERS, ORDERS), :] = dot(hits, high, NT).astype(BF)
        z_low[pl.ds(c * ORDERS, ORDERS), :] = dot(hits, low, NT).astype(BF)
    own = out.shape[0] * S_WIDTH
    first = me[0] * own
    near_order = lax.broadcasted_iota(jnp.int32, (8, S_WIDTH), 0).astype(F32)

    def step(i, carry):
        data = points[:, pl.ds(pl.multiple_of(first + i * S_WIDTH, S_WIDTH), S_WIDTH)]
        hits_here = tile_hits(data[6:7], S_WIDTH)
        picked[...] = dot(z_high[...], hits_here, NN) + dot(z_low[...], hits_here, NN)
        high, low = data[0:1], data[1:2]
        c, s = turn_trig(near_order, high, low)
        c8, s8 = turn_trig(8.0, high, low)
        c8 = jnp.broadcast_to(c8, c.shape)
        s8 = jnp.broadcast_to(s8, c.shape)
        total = None
        for b in range(ORDERS // 8):
            add = c * picked[8 * b : 8 * b + 8, :] + s * picked[ORDERS + 8 * b : ORDERS + 8 * b + 8, :]
            total = add if total is None else total + add
            c, s = c * c8 - s * s8, s * c8 + c * s8
        out[pl.ds(i, 1), :] = jnp.sum(total, axis=0, keepdims=True)
        return carry

    lax.fori_loop(0, out.shape[0], step, 0)


def point_values(me, points, got, extra_row):
    own = points.shape[1] // GROUPS
    return pl.pallas_call(
        lambda *refs: values_kernel(extra_row, *refs),
        out_shape=jax.ShapeDtypeStruct((own // S_WIDTH, S_WIDTH), F32),
        in_specs=[SMEM] + vmem(2),
        out_specs=pl.BlockSpec(memory_space=pltpu.VMEM),
        scratch_shapes=[
            pltpu.VMEM((2 * ORDERS, TILES), BF),
            pltpu.VMEM((2 * ORDERS, TILES), BF),
            pltpu.VMEM((2 * ORDERS, S_WIDTH), F32),
        ],
        compiler_params=params(40),
        cost_estimate=cost(8 * ORDERS * TILES * own, 5 * 10**6),
    )(me, points, got)


def waves():
    k = np.arange(2 * ORDERS)[:, None]
    q = np.arange(HALF)[None, :] * 2 + 1
    phase = 2 * np.pi * ((k * q) % (2 * GRID)) / (2 * GRID)
    out = []
    for f in (np.cos(phase), np.sin(phase)):
        high = f.astype(jnp.bfloat16)
        low = (f - high.astype(np.float64)).astype(jnp.bfloat16)
        out += [high[:ORDERS], low[:ORDERS], high[ORDERS:], low[ORDERS:]]
    return out


def sectoral_values(orders, sines):
    single = (orders == 0.0).astype(F32)
    log_lead = 0.5 * (
        jnp.log(2.0 - single)
        + lax.lgamma(orders + 1.5)
        - lax.lgamma(orders * 0.0 + 1.5)
        - lax.lgamma(orders + 1.0)
    )
    return jnp.exp(log_lead + orders * jnp.log(sines))


def pts_total(x):
    for d in (1, 2, 4, 8):
        x = x + lax.ppermute(x, "pts", [(i, i ^ d) for i in range(16)])
    return x


def swap(x):
    return lax.all_to_all(x, "coef", 0, 0)


def shards(colatitude, longitude, tile_of_point, order_of_slot, observations, obs_weight, prior):
    me = lax.axis_index("coef").astype(jnp.int32).reshape(1)
    local_tile = (tile_of_point - lax.axis_index("pts") * TILES).astype(F32)
    order = order_of_slot.astype(F32)
    orders = jnp.broadcast_to(order[:, None], (SLOTS, LANES))
    cosine = jnp.cos(colatitude)[None, :]
    sectoral = sectoral_values(order[:, None], jnp.sin(colatitude)[None, :])
    degree = np.arange(DEG_PAD, dtype=np.float64)
    scale = jnp.asarray((1.0 / (4 * degree * degree - 1)).astype(np.float32))
    c1, c1l, c2, c2l, s1, s1l, s2, s2l = [jnp.asarray(x) for x in waves()]

    turn = 2.0 * math.pi
    turn_high = 6.28125
    turn_low = turn - turn_high
    high = jnp.round(longitude * (4096.0 / turn)) * (1.0 / 4096.0)
    low = ((longitude - high * turn_high) - high * turn_low) * (1.0 / turn)
    far = high * ORDERS
    far = ((far - jnp.round(far)) + low * ORDERS) * turn
    points = jnp.stack(
        [high, low, obs_weight, obs_weight * observations, jnp.cos(far), jnp.sin(far), local_tile, local_tile]
    )

    field, w_first, w_second = moments(points, orders)
    p_high, p_low = legendre_table(orders, cosine, sectoral, scale)
    prior_row = jnp.pad(prior, (0, DEG_PAD - DEGREES))[None, :]

    residual = pts_total(unfold(field, p_high, p_low, False))
    fourier = fold(residual, p_high, p_low)

    order_row = jnp.concatenate([order, order, jnp.full((LANES - 2 * SLOTS,), -1.0, F32)])[None]

    def extras(*scalars):
        rows = [order_row] + [jnp.full((1, LANES), s, F32) for s in scalars]
        return jnp.concatenate(rows + [jnp.zeros((8 - len(rows), LANES), F32)], 0)

    def everywhere(x):
        return jnp.broadcast_to(x[None], (GROUPS,) + x.shape)

    def by_tiles(x):
        return x.reshape(GROUPS, OWN_TILES, LANES)

    sent = jnp.concatenate(
        [
            everywhere(fourier),
            by_tiles(w_first),
            by_tiles(w_second),
            everywhere(extras(jnp.sum(residual * residual), jnp.sum(prior_row * residual * residual))),
        ],
        1,
    )
    got = swap(sent)
    sums = jnp.sum(got[:, EXTRA_FIRST : EXTRA_FIRST + 8, 0], 0)
    norm_0, prior_00 = sums[1], sums[2]

    back, kept = grid_first(me, got, (c1, c1l, c2, c2l, s1, s1l, s2, s2l))
    seen = swap(back)
    energy_part = jnp.sum(seen[:, OWN_TILES, 0])
    applied = unfold(seen[:, :OWN_TILES].reshape(TILES, LANES), p_high, p_low, True)
    lane = lax.broadcasted_iota(jnp.int32, applied.shape, 1)
    values_0 = point_values(me, points, got, EXTRA_FIRST)
    applied = pts_total(jnp.where(lane == DEGREES, energy_part, applied))
    step_0 = norm_0 / (applied[0, DEGREES] * (INV * INV) + prior_00)
    applied = jnp.where(lane < DEGREES, applied + prior_row * residual, 0.0)
    residual_1 = residual - step_0 * applied

    fourier_1 = fold(residual_1, p_high, p_low)
    got_1 = swap(
        everywhere(
            jnp.concatenate(
                [
                    fourier_1,
                    extras(
                        jnp.sum(residual_1 * residual_1),
                        jnp.sum(prior_row * residual * residual_1),
                        jnp.sum(prior_row * residual_1 * residual_1),
                    ),
                ],
                0,
            )
        )
    )
    sums = jnp.sum(got_1[:, TILES : TILES + 8, 0], 0)
    norm_1, prior_01, prior_11 = sums[1], sums[2], sums[3]
    ratio = norm_1 / norm_0
    energy_1 = pts_total(grid_second(me, ratio.reshape(1), got_1, kept, (c1, c1l, s1, s1l)))
    values_1 = point_values(me, points, got_1, TILES)

    own_rows = values_0.size // LANES
    last = swap(
        everywhere(
            jnp.concatenate(
                [values_0.reshape(own_rows, LANES), values_1.reshape(own_rows, LANES), energy_1], 0
            )
        )
    )
    energy_1 = jnp.sum(last[:, 2 * own_rows, 0])
    curvature = energy_1 * (INV * INV) + prior_11 + 2.0 * ratio * prior_01 + ratio * ratio * prior_00
    step_1 = norm_1 / curvature
    on_0 = step_0 + step_1 * ratio
    vector = on_0 * residual + step_1 * residual_1
    fitted = on_0 * last[:, :own_rows] + step_1 * last[:, own_rows : 2 * own_rows]
    coefficients = vector.reshape(2, SLOTS, DEG_PAD)[:, :, :DEGREES].transpose(2, 0, 1)
    return coefficients, observations - fitted.reshape(-1) * INV


def solution(mesh):
    placed = (P("pts"), P("pts"), P("pts"), P("coef"), P("pts"), P("pts"), P())
    return jax.shard_map(
        shards,
        mesh=mesh,
        in_specs=placed,
        out_specs=(P(None, None, "coef"), P("pts")),
        check_vma=False,
    )
```

```python
import math
import numpy as np
import jax
import jax.numpy as jnp
from jax import lax
from jax.experimental import pallas as pl
from jax.experimental.pallas import tpu as pltpu
from jax.sharding import PartitionSpec as P

DEGREES = 301
DEG_PAD = 304
SLOTS = 40
TILES = 256
GROUPS = 8
OWN_TILES = TILES // GROUPS
ORDERS = 320
GRID = 1280
HALF = GRID // 2
LANES = 128
INV = 1.0 / DEGREES
BF = jnp.bfloat16
F32 = jnp.float32
ROUNDER = 12582912.0

NN = (((1,), (0,)), ((), ()))
NT = (((1,), (1,)), ((), ()))


def fit_even(f, terms):
    r = 0.502 * np.cos((np.arange(400) + 0.5) * np.pi / 800)
    a = np.stack([r ** (2 * k) for k in range(terms)], 1)
    return [float(v) for v in np.linalg.lstsq(a, f(r), rcond=None)[0]]


SIN_TERMS = fit_even(lambda r: np.sin(np.pi * r) / r, 5)
COS_TERMS = fit_even(lambda r: np.cos(np.pi * r), 5)


def horner(x, terms):
    total = terms[-1] * x + terms[-2]
    for term in terms[-3::-1]:
        total = total * x + term
    return total


def turn_trig(order, high, low):
    whole = order * high
    near = (whole + ROUNDER) - ROUNDER
    part = (whole - near) + order * low
    square = part * part
    s = horner(square, SIN_TERMS) * part
    c = horner(square, COS_TERMS)
    twice = s + s
    return 1.0 - twice * s, twice * c


def split(x):
    high = x.astype(BF)
    return high, (x - high.astype(F32)).astype(BF)


def dot(a, b, dims):
    return lax.dot_general(a, b, dims, preferred_element_type=F32)


def mm3(x, b_high, b_low, dims):
    rows = x.shape[0]
    high, low = split(x)
    both = dot(jnp.concatenate([high, low], 0), b_high, dims)
    return both[:rows] + both[rows:] + dot(high, b_low, dims)


def vmem(n):
    return [pl.BlockSpec(memory_space=pltpu.VMEM)] * n


SMEM = pl.BlockSpec(memory_space=pltpu.SMEM)


def params(mib):
    return pltpu.CompilerParams(vmem_limit_bytes=mib * 2**20)


def cost(flops, bytes_accessed):
    return pl.CostEstimate(flops=flops, bytes_accessed=bytes_accessed, transcendentals=0)


def tile_hits(tile_row, width):
    ids = lax.broadcasted_iota(jnp.int32, (TILES, width), 0).astype(F32)
    return jnp.where(ids == tile_row, 1.0, 0.0).astype(BF)


WIDTH = 1024
UNROLL = 2


def moments_kernel(high_r, low_r, weight_r, value_r, c_far_r, s_far_r, tile_r, orders, field, w_first, w_second, total):
    total[...] = jnp.zeros_like(total)
    order = orders[...]

    def make(first):
        parts = []
        for j in range(WIDTH // LANES):
            at = pl.ds(pl.multiple_of(first + j * LANES, LANES), LANES)
            c, s = turn_trig(order, high_r[:, at], low_r[:, at])
            weight, value = weight_r[:, at], value_r[:, at]
            c_far, s_far = c_far_r[:, at], s_far_r[:, at]
            wc, ws = weight * c, weight * s
            rows = jnp.concatenate(
                [value * c, value * s, wc, ws, wc * c_far - ws * s_far, ws * c_far + wc * s_far], 0
            )
            parts.append(split(rows) + (tile_hits(tile_r[:, at], LANES),))
        high, low, hits = [jnp.concatenate(x, 1) for x in zip(*parts)]
        return jnp.concatenate([high, low], 0), hits

    def step(i, carry):
        add = None
        for part in range(UNROLL):
            rows, hits = make((i * UNROLL + part) * WIDTH)
            got = dot(rows, hits, NT)
            add = got if add is None else add + got
        total[...] += add
        return carry

    lax.fori_loop(0, high_r.shape[1] // (WIDTH * UNROLL), step, 0)
    whole = total[0 : 6 * SLOTS] + total[6 * SLOTS : 12 * SLOTS]
    field[...] = whole[0 : 2 * SLOTS]
    blank = jnp.zeros((LANES - 2 * SLOTS, TILES), F32)
    w_first[...] = jnp.concatenate([whole[2 * SLOTS : 4 * SLOTS], blank], 0).T
    w_second[...] = jnp.concatenate([whole[4 * SLOTS : 6 * SLOTS], blank], 0).T


def moments(points, orders):
    n = points[0].shape[1]
    return pl.pallas_call(
        moments_kernel,
        out_shape=[
            jax.ShapeDtypeStruct((2 * SLOTS, TILES), F32),
            jax.ShapeDtypeStruct((TILES, LANES), F32),
            jax.ShapeDtypeStruct((TILES, LANES), F32),
        ],
        in_specs=vmem(8),
        out_specs=vmem(3),
        scratch_shapes=[pltpu.VMEM((12 * SLOTS, TILES), F32)],
        compiler_params=params(12),
        cost_estimate=cost(2 * 12 * SLOTS * TILES * n, 32 * n),
    )(*points, orders)


def table_kernel(orders, cosine, sectoral, scale, p_high, p_low, left, right):
    order = jnp.broadcast_to(orders[:, 0:1], (SLOTS, TILES))
    order_sq = orders[...] * orders[...]
    cos_row = jnp.broadcast_to(cosine[...], (SLOTS, TILES))
    start = sectoral[...]

    def put(n, value):
        for b in range(SLOTS // 8):
            at = pl.ds(b * 8 * DEG_PAD + n, 8, stride=DEG_PAD)
            left[at, :] = value[8 * b : 8 * b + 8, 0:LANES]
            right[at, :] = value[8 * b : 8 * b + 8, LANES:TILES]

    def step(n, carried):
        recent, earlier, back = carried
        degree = n.astype(F32)
        ratio = jnp.maximum((degree * degree - order_sq) * scale[n], 1e-20)
        up = lax.rsqrt(ratio)
        this_back = ratio * up
        up2 = jnp.concatenate([up, up], 1)
        back2 = jnp.concatenate([back, back], 1)
        grown = up2 * (cos_row * recent - back2 * earlier)
        value = jnp.where(order > degree, 0.0, jnp.where(order == degree, start, grown))
        put(n, value)
        return value, recent, this_back

    empty = jnp.zeros((SLOTS, TILES), F32)
    unset = start * 0.0
    lax.fori_loop(0, DEG_PAD, step, (unset, unset, order_sq * 0.0), unroll=4)
    for n in range(DEGREES, DEG_PAD):
        put(n, empty)

    def pack(slot, carry):
        at = pl.ds(pl.multiple_of(slot * DEG_PAD, 8), DEG_PAD)
        high, low = split(jnp.concatenate([left[at, :], right[at, :]], 1))
        p_high[slot] = high
        p_low[slot] = low
        return carry

    lax.fori_loop(0, SLOTS, pack, 0)


def legendre_table(orders, cosine, sectoral, scale):
    shape = jax.ShapeDtypeStruct((SLOTS, DEG_PAD, TILES), BF)
    return pl.pallas_call(
        table_kernel,
        out_shape=[shape, shape],
        in_specs=vmem(3) + [SMEM],
        out_specs=vmem(2),
        scratch_shapes=[pltpu.VMEM((SLOTS * DEG_PAD, LANES), F32)] * 2,
        compiler_params=params(16),
        cost_estimate=cost(20 * SLOTS * DEG_PAD * TILES, 4 * SLOTS * DEG_PAD * TILES),
    )(orders, cosine, sectoral, scale)


def by_slot(vector, p_high, p_low, width, dims, put):
    row = lax.broadcasted_iota(jnp.int32, (16, width), 0)

    def group(g, carry):
        at = pl.multiple_of(g * 8, 8)
        rows = jnp.concatenate([vector[pl.ds(at, 8), :], vector[pl.ds(at + SLOTS, 8), :]], 0)
        high, low = split(rows)
        both = jnp.concatenate([high, low], 0)
        out = jnp.zeros((16, width), F32)
        for i in range(8):
            first = dot(both, p_high[at + i], dims)
            total = first[0:16] + first[16:32] + dot(high, p_low[at + i], dims)
            out = jnp.where((row == i) | (row == i + 8), total, out)
        put(at, out)
        return carry

    lax.fori_loop(0, SLOTS // 8, group, 0)


EXTRA_FIRST = TILES + 2 * OWN_TILES


def all_sum(x):
    return jnp.sum(jnp.sum(x, axis=1, keepdims=True), axis=0, keepdims=True)


def extra_rows(order_row, sums):
    rows = [order_row] + [jnp.broadcast_to(x, (1, LANES)) for x in sums]
    return jnp.concatenate(rows + [jnp.zeros((8 - len(rows), LANES), F32)], 0)


def source_sum(got, row):
    total = got[0, row : row + 1, 0:1]
    for g in range(1, GROUPS):
        total = total + got[g, row : row + 1, 0:1]
    return total


def fold_into(vector, p_high, p_low, rows):
    def put(at, value):
        rows[pl.ds(at, 8), :] = value[0:8]
        rows[pl.ds(at + SLOTS, 8), :] = value[8:16]

    rows[2 * SLOTS :, :] = jnp.zeros((LANES - 2 * SLOTS, TILES), F32)
    by_slot(vector, p_high, p_low, TILES, NN, put)
    return rows[...].T


def fold_first_kernel(vector, p_high, p_low, prior, order_row, w_first, w_second, sent, rows):
    folded = fold_into(vector, p_high, p_low, rows)
    v = vector[...]
    extra = extra_rows(order_row[...], [all_sum(v * v), all_sum(prior[...] * v * v)])
    t = OWN_TILES
    for g in range(GROUPS):
        sent[g, 0:TILES, :] = folded
        sent[g, TILES : TILES + t, :] = w_first[g * t : (g + 1) * t, :]
        sent[g, TILES + t : TILES + 2 * t, :] = w_second[g * t : (g + 1) * t, :]
        sent[g, EXTRA_FIRST : EXTRA_FIRST + 8, :] = extra


def fold_first(vector, p_high, p_low, prior, order_row, w_first, w_second):
    return pl.pallas_call(
        fold_first_kernel,
        out_shape=jax.ShapeDtypeStruct((GROUPS, EXTRA_FIRST + 8, LANES), F32),
        in_specs=vmem(7),
        out_specs=pl.BlockSpec(memory_space=pltpu.VMEM),
        scratch_shapes=[pltpu.VMEM((LANES, TILES), F32)],
        compiler_params=params(8),
        cost_estimate=cost(64 * SLOTS * DEG_PAD * TILES, 4 * SLOTS * DEG_PAD * TILES),
    )(vector, p_high, p_low, prior, order_row, w_first, w_second)


def fold_second_kernel(vector, applied, got, p_high, p_low, prior, order_row, sent, next_vector, step, rows):
    v = vector[...]
    lane = lax.broadcasted_iota(jnp.int32, v.shape, 1)
    norm = source_sum(got, EXTRA_FIRST + 1)
    weighed = source_sum(got, EXTRA_FIRST + 2)
    alpha = norm / (applied[0:1, DEGREES : DEGREES + 1] * (INV * INV) + weighed)
    r = v - alpha * jnp.where(lane < DEGREES, applied[...] + prior[...] * v, 0.0)
    next_vector[...] = r
    step[...] = jnp.concatenate(
        [jnp.broadcast_to(x, (1, LANES)) for x in (alpha, norm, weighed)] + [jnp.zeros((5, LANES), F32)], 0
    )
    folded = fold_into(next_vector, p_high, p_low, rows)
    extra = extra_rows(
        order_row[...], [all_sum(r * r), all_sum(prior[...] * v * r), all_sum(prior[...] * r * r)]
    )
    for g in range(GROUPS):
        sent[g, 0:TILES, :] = folded
        sent[g, TILES : TILES + 8, :] = extra


def fold_second(vector, applied, got, p_high, p_low, prior, order_row):
    return pl.pallas_call(
        fold_second_kernel,
        out_shape=[
            jax.ShapeDtypeStruct((GROUPS, TILES + 8, LANES), F32),
            jax.ShapeDtypeStruct((2 * SLOTS, DEG_PAD), F32),
            jax.ShapeDtypeStruct((8, LANES), F32),
        ],
        in_specs=vmem(7),
        out_specs=vmem(3),
        scratch_shapes=[pltpu.VMEM((LANES, TILES), F32)],
        compiler_params=params(8),
        cost_estimate=cost(64 * SLOTS * DEG_PAD * TILES, 4 * SLOTS * DEG_PAD * TILES),
    )(vector, applied, got, p_high, p_low, prior, order_row)


def unfold_first_kernel(field, p_high, p_low, out):
    def put(at, value):
        out[pl.ds(at, 8), :] = value[0:8] * INV
        out[pl.ds(at + SLOTS, 8), :] = value[8:16] * INV

    by_slot(field, p_high, p_low, DEG_PAD, NT, put)


def unfold_second_kernel(seen, p_high, p_low, out, rows):
    t = OWN_TILES
    rows[...] = jnp.concatenate([seen[g, 0:t, :] for g in range(GROUPS)], 0).T
    energy = source_sum(seen, t)
    lane = lax.broadcasted_iota(jnp.int32, (8, DEG_PAD), 1)

    def put(at, value):
        out[pl.ds(at, 8), :] = jnp.where(lane == DEGREES, energy, value[0:8] * (INV * INV))
        out[pl.ds(at + SLOTS, 8), :] = value[8:16] * (INV * INV)

    by_slot(rows, p_high, p_low, DEG_PAD, NT, put)


def unfold(field, p_high, p_low, second):
    return pl.pallas_call(
        unfold_second_kernel if second else unfold_first_kernel,
        out_shape=jax.ShapeDtypeStruct((2 * SLOTS, DEG_PAD), F32),
        in_specs=vmem(3),
        out_specs=pl.BlockSpec(memory_space=pltpu.VMEM),
        scratch_shapes=[pltpu.VMEM((LANES, TILES), F32)] if second else [],
        compiler_params=params(8),
        cost_estimate=cost(64 * SLOTS * DEG_PAD * TILES, 4 * SLOTS * DEG_PAD * TILES),
    )(field, p_high, p_low)


def slot_hits(order_row):
    wanted = lax.broadcasted_iota(jnp.int32, (ORDERS, LANES), 0).astype(F32)
    return jnp.where(wanted == order_row, 1.0, 0.0).astype(BF)


def two_halves(x):
    lane = lax.broadcasted_iota(jnp.int32, x.shape, 1)
    return jnp.where(lane < SLOTS, x, 0.0), jnp.where((lane >= SLOTS) & (lane < 2 * SLOTS), x, 0.0)


def to_natural(pieces, hits):
    total = None
    for per_source, hit in zip(pieces, hits):
        rows = [half for x in per_source for half in two_halves(x)]
        high, low = split(jnp.concatenate(rows, 0))
        got = dot(jnp.concatenate([high, low], 0), hit, NT)
        total = got if total is None else total + got
    n = total.shape[0] // 2
    return total[:n] + total[n:]


def grid_first_kernel(me, got, c1, c1l, c2, c2l, s1, s1l, s2, s2l, back, kept):
    mine = pl.multiple_of(me[0] * OWN_TILES, OWN_TILES)
    t = OWN_TILES
    hits = [slot_hits(got[g, EXTRA_FIRST : EXTRA_FIRST + 1, :]) for g in range(GROUPS)]
    nat = to_natural(
        [
            [got[g, pl.ds(mine, t), :], got[g, TILES : TILES + t, :], got[g, TILES + t : TILES + 2 * t, :]]
            for g in range(GROUPS)
        ],
        hits,
    )
    k = lax.broadcasted_iota(jnp.int32, (1, ORDERS), 1)
    k_first = jnp.where(k == 0, 1.0 / GRID, 2.0 / GRID)
    k_second = jnp.where(k + ORDERS <= 2 * (DEGREES - 1), 2.0 / GRID, 0.0)
    even = mm3(jnp.concatenate([nat[0:t], nat[2 * t : 3 * t] * k_first], 0), c1[...], c1l[...], NN)
    odd = mm3(jnp.concatenate([nat[t : 2 * t], nat[3 * t : 4 * t] * k_first], 0), s1[...], s1l[...], NN)
    w_even = even[t:] + mm3(nat[4 * t : 5 * t] * k_second, c2[...], c2l[...], NN)
    w_odd = odd[t:] + mm3(nat[5 * t : 6 * t] * k_second, s2[...], s2l[...], NN)
    even, odd = even[:t], odd[:t]
    h_even = 2.0 * (w_even * even + w_odd * odd)
    h_odd = 2.0 * (w_even * odd + w_odd * even)
    energy = all_sum(h_even * even + h_odd * odd)
    kept[0] = even
    kept[1] = odd
    kept[2] = w_even
    kept[3] = w_odd
    hc = mm3(h_even, c1[...], c1l[...], NT)
    hs = mm3(h_odd, s1[...], s1l[...], NT)
    c_high, c_low = split(hc)
    s_high, s_low = split(hs)
    stack = jnp.concatenate([c_high, c_low, s_high, s_low], 0)
    lane = lax.broadcasted_iota(jnp.int32, (t, LANES), 1)
    for g in range(GROUPS):
        slots = dot(stack, hits[g], NN)
        back[g, 0:t, :] = jnp.where(
            lane < SLOTS, slots[0:t] + slots[t : 2 * t], slots[2 * t : 3 * t] + slots[3 * t :]
        )
        back[g, t : t + 8, :] = jnp.broadcast_to(energy, (8, LANES))


def grid_first(me, got, waves):
    return pl.pallas_call(
        grid_first_kernel,
        out_shape=[
            jax.ShapeDtypeStruct((GROUPS, OWN_TILES + 8, LANES), F32),
            jax.ShapeDtypeStruct((4, OWN_TILES, HALF), F32),
        ],
        in_specs=[SMEM] + vmem(9),
        out_specs=vmem(2),
        compiler_params=params(8),
        cost_estimate=cost(10**9, 5 * 10**6),
    )(me, got, *waves)


def grid_second_kernel(me, step, got, kept, c1, c1l, s1, s1l, out):
    mine = pl.multiple_of(me[0] * OWN_TILES, OWN_TILES)
    t = OWN_TILES
    hits = [slot_hits(got[g, TILES : TILES + 1, :]) for g in range(GROUPS)]
    nat = to_natural([[got[g, pl.ds(mine, t), :]] for g in range(GROUPS)], hits)
    ratio = source_sum(got, TILES + 1) / step[1:2, 0:1]
    even = mm3(nat[0:t], c1[...], c1l[...], NN) + ratio * kept[0]
    odd = mm3(nat[t:], s1[...], s1l[...], NN) + ratio * kept[1]
    w_even, w_odd = kept[2], kept[3]
    terms = 2.0 * w_even * (even * even + odd * odd) + 4.0 * w_odd * (even * odd)
    energy = all_sum(terms)
    out[...] = jnp.broadcast_to(energy, (8, LANES))


def grid_second(me, step, got, kept, waves):
    return pl.pallas_call(
        grid_second_kernel,
        out_shape=jax.ShapeDtypeStruct((8, LANES), F32),
        in_specs=[SMEM] + vmem(7),
        out_specs=pl.BlockSpec(memory_space=pltpu.VMEM),
        compiler_params=params(8),
        cost_estimate=cost(10**9, 5 * 10**6),
    )(me, step, got, kept, *waves)


S_WIDTH = 512


def lookup_kernel(extra_row, got, z_high, z_low):
    hits = jnp.concatenate(
        [slot_hits(got[g, extra_row : extra_row + 1, :]) for g in range(GROUPS)], 1
    )
    halves = [two_halves(got[g, 0:TILES, :]) for g in range(GROUPS)]
    for c in range(2):
        high, low = split(jnp.concatenate([h[c] for h in halves], 1))
        z_high[pl.ds(c * ORDERS, ORDERS), :] = dot(hits, high, NT).astype(BF)
        z_low[pl.ds(c * ORDERS, ORDERS), :] = dot(hits, low, NT).astype(BF)


def lookup(got, extra_row):
    shape = jax.ShapeDtypeStruct((2 * ORDERS, TILES), BF)
    return pl.pallas_call(
        lambda *refs: lookup_kernel(extra_row, *refs),
        out_shape=[shape, shape],
        in_specs=vmem(1),
        out_specs=vmem(2),
        compiler_params=params(10),
        cost_estimate=cost(10**9, 3 * 10**6),
    )(got)


def values_kernel(start, me, high_r, low_r, tile_r, z_high, z_low, out):
    first = me[0] * (high_r.shape[1] // GROUPS) + start * S_WIDTH
    near_order = lax.broadcasted_iota(jnp.int32, (8, S_WIDTH), 0).astype(F32)

    def step(i, carry):
        at = pl.ds(pl.multiple_of(first + i * S_WIDTH, S_WIDTH), S_WIDTH)
        hits_here = tile_hits(tile_r[:, at], S_WIDTH)
        picked = dot(z_high[...], hits_here, NN) + dot(z_low[...], hits_here, NN)
        high, low = high_r[:, at], low_r[:, at]
        c, s = turn_trig(near_order, high, low)
        c8, s8 = turn_trig(8.0, high, low)
        c8 = jnp.broadcast_to(c8, c.shape)
        s8 = jnp.broadcast_to(s8, c.shape)
        total = None
        for b in range(ORDERS // 8):
            add = c * picked[8 * b : 8 * b + 8, :] + s * picked[ORDERS + 8 * b : ORDERS + 8 * b + 8, :]
            total = add if total is None else total + add
            c, s = c * c8 - s * s8, s * c8 + c * s8
        out[pl.ds(i, 1), :] = jnp.sum(total, axis=0, keepdims=True)
        return carry

    lax.fori_loop(0, out.shape[0], step, 0)


def point_values(me, points, tables, start, rows):
    high, low, tile = points
    return pl.pallas_call(
        lambda *refs: values_kernel(start, *refs),
        out_shape=jax.ShapeDtypeStruct((rows, S_WIDTH), F32),
        in_specs=[SMEM] + vmem(5),
        out_specs=pl.BlockSpec(memory_space=pltpu.VMEM),
        compiler_params=params(10),
        cost_estimate=cost(8 * ORDERS * TILES * rows * S_WIDTH, 10**6),
    )(me, high, low, tile, *tables)


def final_kernel(last, step, got, vector, next_vector, observed, fitted, coefficients):
    rows = fitted.shape[1]
    alpha, norm, prior_00 = step[0:1, 0:1], step[1:2, 0:1], step[2:3, 0:1]
    norm_1 = source_sum(got, TILES + 1)
    prior_01 = source_sum(got, TILES + 2)
    prior_11 = source_sum(got, TILES + 3)
    energy = source_sum(last, 2 * rows)
    ratio = norm_1 / norm
    curvature = energy * (INV * INV) + prior_11 + 2.0 * ratio * prior_01 + ratio * ratio * prior_00
    beta = norm_1 / curvature
    on_first = alpha + beta * ratio
    coefficients[...] = on_first * vector[...] + beta * next_vector[...]
    on_first, beta = on_first * INV, beta * INV
    for g in range(GROUPS):
        fitted[g] = observed[g] - (on_first * last[g, 0:rows, :] + beta * last[g, rows : 2 * rows, :])


def final(last, step, got, vector, next_vector, observed):
    return pl.pallas_call(
        final_kernel,
        out_shape=[
            jax.ShapeDtypeStruct(observed.shape, F32),
            jax.ShapeDtypeStruct(vector.shape, F32),
        ],
        in_specs=vmem(6),
        out_specs=vmem(2),
        compiler_params=params(8),
        cost_estimate=cost(10**7, 3 * 10**6),
    )(last, step, got, vector, next_vector, observed)


def waves():
    k = np.arange(2 * ORDERS)[:, None]
    q = np.arange(HALF)[None, :] * 2 + 1
    phase = 2 * np.pi * ((k * q) % (2 * GRID)) / (2 * GRID)
    out = []
    for f in (np.cos(phase), np.sin(phase)):
        high = f.astype(jnp.bfloat16)
        low = (f - high.astype(np.float64)).astype(jnp.bfloat16)
        out += [high[:ORDERS], low[:ORDERS], high[ORDERS:], low[ORDERS:]]
    return out


def sectoral_values(orders, sines):
    single = (orders == 0.0).astype(F32)
    log_lead = 0.5 * (
        jnp.log(2.0 - single)
        + lax.lgamma(orders + 1.5)
        - lax.lgamma(orders * 0.0 + 1.5)
        - lax.lgamma(orders + 1.0)
    )
    return jnp.exp(log_lead + orders * jnp.log(sines))


def pts_total(x, beside=()):
    made = []
    for k, d in enumerate((1, 2, 4, 8)):
        task = beside[k] if k < len(beside) else None
        gate = jnp.zeros((1,), jnp.int32)
        if task is not None:
            x, gate = lax.optimization_barrier((x, gate))
        other = lax.ppermute(x, "pts", [(i, i ^ d) for i in range(16)])
        if task is not None:
            out = task(gate)
            other, out = lax.optimization_barrier((other, out))
            made.append(out)
        x = x + other
    return x, made


def swap(x):
    return lax.all_to_all(x, "coef", 0, 0)


def shards(colatitude, longitude, tile_of_point, order_of_slot, observations, obs_weight, prior):
    me = lax.axis_index("coef").astype(jnp.int32).reshape(1)
    local_tile = (tile_of_point - lax.axis_index("pts") * TILES).astype(F32)
    order = order_of_slot.astype(F32)
    orders = jnp.broadcast_to(order[:, None], (SLOTS, LANES))
    cosine = jnp.cos(colatitude)[None, :]
    sectoral = sectoral_values(order[:, None], jnp.sin(colatitude)[None, :])
    degree = np.arange(DEG_PAD, dtype=np.float64)
    scale = jnp.asarray((1.0 / (4 * degree * degree - 1)).astype(np.float32))
    c1, c1l, c2, c2l, s1, s1l, s2, s2l = [jnp.asarray(x) for x in waves()]

    turn = 2.0 * math.pi
    turn_high = 6.28125
    turn_low = turn - turn_high
    high = jnp.round(longitude * (4096.0 / turn)) * (1.0 / 4096.0)
    low = ((longitude - high * turn_high) - high * turn_low) * (1.0 / turn)
    far = high * ORDERS
    far = ((far - jnp.round(far)) + low * ORDERS) * turn
    weighted = obs_weight * observations
    points = [x[None] for x in (high, low, obs_weight, weighted, jnp.cos(far), jnp.sin(far), local_tile)]
    near = points[0], points[1], points[6]

    field, w_first, w_second = moments(points, orders)
    p_high, p_low = legendre_table(orders, cosine, sectoral, scale)
    prior_row = jnp.pad(prior, (0, DEG_PAD - DEGREES))[None, :]
    order_row = jnp.concatenate([order, order, jnp.full((LANES - 2 * SLOTS,), -1.0, F32)])[None]
    own_rows = high.shape[0] // (GROUPS * S_WIDTH)
    half = own_rows // 2

    residual, _ = pts_total(unfold(field, p_high, p_low, False))
    got = swap(fold_first(residual, p_high, p_low, prior_row, order_row, w_first, w_second))

    back, kept = grid_first(me, got, (c1, c1l, c2, c2l, s1, s1l, s2, s2l))
    tables_0 = lookup(got, EXTRA_FIRST)
    back, me_0 = lax.optimization_barrier((back, me))
    seen = swap(back)
    values_00 = point_values(me_0, near, tables_0, 0, half)
    seen, values_00 = lax.optimization_barrier((seen, values_00))
    applied, (values_01,) = pts_total(
        unfold(seen, p_high, p_low, True),
        [None, None, lambda gate: point_values(me + gate, near, tables_0, half, own_rows - half)],
    )
    sent_1, residual_1, step = fold_second(residual, applied, got, p_high, p_low, prior_row, order_row)
    got_1 = swap(sent_1)
    part = grid_second(me, step, got_1, kept, (c1, c1l, s1, s1l))
    tables_1 = lookup(got_1, TILES)
    third = own_rows // 3
    energy_1, values_1 = pts_total(
        part,
        [
            None,
            lambda gate: point_values(me + gate, near, tables_1, 0, third),
            lambda gate: point_values(me + gate, near, tables_1, third, third),
            lambda gate: point_values(me + gate, near, tables_1, 2 * third, own_rows - 2 * third),
        ],
    )
    payload = jnp.concatenate(
        [x.reshape(-1, LANES) for x in [values_00, values_01] + values_1] + [energy_1], 0
    )
    last = swap(jnp.broadcast_to(payload[None], (GROUPS,) + payload.shape))
    residual_out, vector = final(
        last, step, got_1, residual, residual_1, observations.reshape(GROUPS, -1, LANES)
    )
    coefficients = vector.reshape(2, SLOTS, DEG_PAD)[:, :, :DEGREES].transpose(2, 0, 1)
    return coefficients, residual_out.reshape(-1)


def solution(mesh):
    placed = (P("pts"), P("pts"), P("pts"), P("coef"), P("pts"), P("pts"), P())
    return jax.shard_map(
        shards,
        mesh=mesh,
        in_specs=placed,
        out_specs=(P(None, None, "coef"), P("pts")),
        check_vma=False,
    )
```

```python
import math
import numpy as np
import jax
import jax.numpy as jnp
from jax import lax
from jax.experimental import pallas as pl
from jax.experimental.pallas import tpu as pltpu
from jax.sharding import PartitionSpec as P

DEGREES = 301
DEG_PAD = 304
SLOTS = 40
TILES = 256
GROUPS = 8
OWN_TILES = TILES // GROUPS
ORDERS = 320
GRID = 1280
HALF = GRID // 2
LANES = 128
INV = 1.0 / DEGREES
BF = jnp.bfloat16
F32 = jnp.float32
ROUNDER = 12582912.0

NN = (((1,), (0,)), ((), ()))
NT = (((1,), (1,)), ((), ()))


def fit_even(f, terms):
    r = 0.502 * np.cos((np.arange(400) + 0.5) * np.pi / 800)
    a = np.stack([r ** (2 * k) for k in range(terms)], 1)
    return [float(v) for v in np.linalg.lstsq(a, f(r), rcond=None)[0]]


SIN_TERMS = fit_even(lambda r: np.sin(np.pi * r) / r, 5)
COS_TERMS = fit_even(lambda r: np.cos(np.pi * r), 5)


def horner(x, terms):
    total = terms[-1] * x + terms[-2]
    for term in terms[-3::-1]:
        total = total * x + term
    return total


def turn_trig(order, high, low):
    whole = order * high
    near = (whole + ROUNDER) - ROUNDER
    part = (whole - near) + order * low
    square = part * part
    s = horner(square, SIN_TERMS) * part
    c = horner(square, COS_TERMS)
    twice = s + s
    return 1.0 - twice * s, twice * c


def split(x):
    high = x.astype(BF)
    return high, (x - high.astype(F32)).astype(BF)


def dot(a, b, dims):
    return lax.dot_general(a, b, dims, preferred_element_type=F32)


def mm3(x, b_high, b_low, dims):
    rows = x.shape[0]
    high, low = split(x)
    both = dot(jnp.concatenate([high, low], 0), b_high, dims)
    return both[:rows] + both[rows:] + dot(high, b_low, dims)


def vmem(n):
    return [pl.BlockSpec(memory_space=pltpu.VMEM)] * n


SMEM = pl.BlockSpec(memory_space=pltpu.SMEM)


def params(mib):
    return pltpu.CompilerParams(vmem_limit_bytes=mib * 2**20)


def cost(flops, bytes_accessed):
    return pl.CostEstimate(flops=flops, bytes_accessed=bytes_accessed, transcendentals=0)


def tile_hits(tile_row, width):
    ids = lax.broadcasted_iota(jnp.int32, (TILES, width), 0).astype(F32)
    return jnp.where(ids == tile_row, 1.0, 0.0).astype(BF)


WIDTH = 1024
UNROLL = 4


def moments_kernel(high_r, low_r, weight_r, value_r, c_far_r, s_far_r, tile_r, orders, field, w_first, w_second, total):
    total[...] = jnp.zeros_like(total)
    order = orders[...]

    def make(first):
        parts = []
        for j in range(WIDTH // LANES):
            at = pl.ds(pl.multiple_of(first + j * LANES, LANES), LANES)
            c, s = turn_trig(order, high_r[:, at], low_r[:, at])
            weight, value = weight_r[:, at], value_r[:, at]
            c_far, s_far = c_far_r[:, at], s_far_r[:, at]
            wc, ws = weight * c, weight * s
            rows = jnp.concatenate(
                [value * c, value * s, wc, ws, wc * c_far - ws * s_far, ws * c_far + wc * s_far], 0
            )
            parts.append(split(rows) + (tile_hits(tile_r[:, at], LANES),))
        high, low, hits = [jnp.concatenate(x, 1) for x in zip(*parts)]
        return jnp.concatenate([high, low], 0), hits

    def step(i, carry):
        add = None
        for part in range(UNROLL):
            rows, hits = make((i * UNROLL + part) * WIDTH)
            got = dot(rows, hits, NT)
            add = got if add is None else add + got
        total[...] += add
        return carry

    lax.fori_loop(0, high_r.shape[1] // (WIDTH * UNROLL), step, 0)
    whole = total[0 : 6 * SLOTS] + total[6 * SLOTS : 12 * SLOTS]
    field[...] = whole[0 : 2 * SLOTS]
    blank = jnp.zeros((LANES - 2 * SLOTS, TILES), F32)
    w_first[...] = jnp.concatenate([whole[2 * SLOTS : 4 * SLOTS], blank], 0).T
    w_second[...] = jnp.concatenate([whole[4 * SLOTS : 6 * SLOTS], blank], 0).T


def moments(points, orders):
    n = points[0].shape[1]
    return pl.pallas_call(
        moments_kernel,
        out_shape=[
            jax.ShapeDtypeStruct((2 * SLOTS, TILES), F32),
            jax.ShapeDtypeStruct((TILES, LANES), F32),
            jax.ShapeDtypeStruct((TILES, LANES), F32),
        ],
        in_specs=vmem(8),
        out_specs=vmem(3),
        scratch_shapes=[pltpu.VMEM((12 * SLOTS, TILES), F32)],
        compiler_params=params(12),
        cost_estimate=cost(2 * 12 * SLOTS * TILES * n, 32 * n),
    )(*points, orders)


def table_kernel(orders, cosine, sectoral, scale, p_high, p_low, left, right):
    order = jnp.broadcast_to(orders[:, 0:1], (SLOTS, TILES))
    order_sq = orders[...] * orders[...]
    cos_row = jnp.broadcast_to(cosine[...], (SLOTS, TILES))
    start = sectoral[...]

    def put(n, value):
        for b in range(SLOTS // 8):
            at = pl.ds(b * 8 * DEG_PAD + n, 8, stride=DEG_PAD)
            left[at, :] = value[8 * b : 8 * b + 8, 0:LANES]
            right[at, :] = value[8 * b : 8 * b + 8, LANES:TILES]

    def step(n, carried):
        recent, earlier, back = carried
        degree = n.astype(F32)
        ratio = jnp.maximum((degree * degree - order_sq) * scale[n], 1e-20)
        up = lax.rsqrt(ratio)
        this_back = ratio * up
        up2 = jnp.concatenate([up, up], 1)
        back2 = jnp.concatenate([back, back], 1)
        grown = up2 * (cos_row * recent - back2 * earlier)
        value = jnp.where(order > degree, 0.0, jnp.where(order == degree, start, grown))
        put(n, value)
        return value, recent, this_back

    empty = jnp.zeros((SLOTS, TILES), F32)
    unset = start * 0.0
    lax.fori_loop(0, DEG_PAD, step, (unset, unset, order_sq * 0.0), unroll=4)
    for n in range(DEGREES, DEG_PAD):
        put(n, empty)

    def pack(slot, carry):
        at = pl.ds(pl.multiple_of(slot * DEG_PAD, 8), DEG_PAD)
        high, low = split(jnp.concatenate([left[at, :], right[at, :]], 1))
        p_high[slot] = high
        p_low[slot] = low
        return carry

    lax.fori_loop(0, SLOTS, pack, 0)


def legendre_table(orders, cosine, sectoral, scale):
    shape = jax.ShapeDtypeStruct((SLOTS, DEG_PAD, TILES), BF)
    return pl.pallas_call(
        table_kernel,
        out_shape=[shape, shape],
        in_specs=vmem(3) + [SMEM],
        out_specs=vmem(2),
        scratch_shapes=[pltpu.VMEM((SLOTS * DEG_PAD, LANES), F32)] * 2,
        compiler_params=params(16),
        cost_estimate=cost(20 * SLOTS * DEG_PAD * TILES, 4 * SLOTS * DEG_PAD * TILES),
    )(orders, cosine, sectoral, scale)


def slot_group(vector, at, high_of, low_of, width, dims):
    row = lax.broadcasted_iota(jnp.int32, (16, width), 0)
    rows = jnp.concatenate([vector[pl.ds(at, 8), :], vector[pl.ds(at + SLOTS, 8), :]], 0)
    high, low = split(rows)
    both = jnp.concatenate([high, low], 0)
    out = jnp.zeros((16, width), F32)
    for i in range(8):
        first = dot(both, high_of(at + i), dims)
        total = first[0:16] + first[16:32] + dot(high, low_of(at + i), dims)
        out = jnp.where((row == i) | (row == i + 8), total, out)
    return out


def by_slot(vector, p_high, p_low, width, dims, put, ready=None):
    def group(g, carry):
        at = pl.multiple_of(g * 8, 8)
        if ready is not None:
            ready(g)
        put(at, slot_group(vector, at, lambda i: p_high[i], lambda i: p_low[i], width, dims))
        return carry

    lax.fori_loop(0, SLOTS // 8, group, 0)


F_ROWS = 2 * SLOTS
EXTRA_FIRST = F_ROWS + OWN_TILES
EXTRA_SECOND = F_ROWS


def all_sum(x):
    return jnp.sum(jnp.sum(x, axis=1, keepdims=True), axis=0, keepdims=True)


def extra_rows(order_row, sums):
    rows = [order_row] + [jnp.broadcast_to(x, (1, LANES)) for x in sums]
    rows = jnp.concatenate(rows + [jnp.zeros((8 - len(rows), LANES), F32)], 0)
    return jnp.concatenate([rows, rows], 1)


def source_sum(got, row):
    total = got[0, row : row + 1, 0:1]
    for g in range(1, GROUPS):
        total = total + got[g, row : row + 1, 0:1]
    return total


def fold_into(vector, p_high, p_low, rows):
    def put(at, value):
        rows[pl.ds(at, 8), :] = value[0:8]
        rows[pl.ds(at + SLOTS, 8), :] = value[8:16]

    by_slot(vector, p_high, p_low, TILES, NN, put)
    return rows[...]


def join(core, mine, other):
    even = core[0] == 0
    mine, other = mine[...], other[...]
    return jnp.concatenate([jnp.where(even, mine, other), jnp.where(even, other, mine)], 0)


def fold_first_kernel(core, mine, other, p_high, p_low, prior, order_row, w_first, w_second, sent, vector, rows):
    v = join(core, mine, other)
    vector[...] = v
    folded = fold_into(vector, p_high, p_low, rows)
    extra = extra_rows(order_row[...], [all_sum(v * v), all_sum(prior[...] * v * v)])
    t = OWN_TILES
    for g in range(GROUPS):
        sent[g, 0:F_ROWS, :] = folded
        sent[g, F_ROWS:EXTRA_FIRST, 0:LANES] = w_first[g * t : (g + 1) * t, :]
        sent[g, F_ROWS:EXTRA_FIRST, LANES:TILES] = w_second[g * t : (g + 1) * t, :]
        sent[g, EXTRA_FIRST : EXTRA_FIRST + 8, :] = extra


def fold_first(core, halves, p_high, p_low, prior, order_row, w_first, w_second):
    return pl.pallas_call(
        fold_first_kernel,
        out_shape=[
            jax.ShapeDtypeStruct((GROUPS, EXTRA_FIRST + 8, TILES), F32),
            jax.ShapeDtypeStruct((2 * SLOTS, DEG_PAD), F32),
        ],
        in_specs=[SMEM] + vmem(8),
        out_specs=vmem(2),
        scratch_shapes=[pltpu.VMEM((2 * SLOTS, TILES), F32)],
        compiler_params=params(8),
        cost_estimate=cost(64 * SLOTS * DEG_PAD * TILES, 4 * SLOTS * DEG_PAD * TILES),
    )(core, *halves, p_high, p_low, prior, order_row, w_first, w_second)


def fold_second_kernel(core, mine, other, vector, got, p_high, p_low, prior, order_row, sent, next_vector, step, rows):
    v = vector[...]
    applied = join(core, mine, other)
    lane = lax.broadcasted_iota(jnp.int32, v.shape, 1)
    norm = source_sum(got, EXTRA_FIRST + 1)
    weighed = source_sum(got, EXTRA_FIRST + 2)
    alpha = norm / (applied[0:1, DEGREES : DEGREES + 1] * (INV * INV) + weighed)
    r = v - alpha * jnp.where(lane < DEGREES, applied + prior[...] * v, 0.0)
    next_vector[...] = r
    step[...] = jnp.concatenate(
        [jnp.broadcast_to(x, (1, LANES)) for x in (alpha, norm, weighed)] + [jnp.zeros((5, LANES), F32)], 0
    )
    folded = fold_into(next_vector, p_high, p_low, rows)
    extra = extra_rows(
        order_row[...], [all_sum(r * r), all_sum(prior[...] * v * r), all_sum(prior[...] * r * r)]
    )
    for g in range(GROUPS):
        sent[g, 0:F_ROWS, :] = folded
        sent[g, EXTRA_SECOND : EXTRA_SECOND + 8, :] = extra


def fold_second(core, halves, vector, got, p_high, p_low, prior, order_row):
    return pl.pallas_call(
        fold_second_kernel,
        out_shape=[
            jax.ShapeDtypeStruct((GROUPS, EXTRA_SECOND + 8, TILES), F32),
            jax.ShapeDtypeStruct((2 * SLOTS, DEG_PAD), F32),
            jax.ShapeDtypeStruct((8, LANES), F32),
        ],
        in_specs=[SMEM] + vmem(8),
        out_specs=vmem(3),
        scratch_shapes=[pltpu.VMEM((2 * SLOTS, TILES), F32)],
        compiler_params=params(8),
        cost_estimate=cost(64 * SLOTS * DEG_PAD * TILES, 4 * SLOTS * DEG_PAD * TILES),
    )(core, *halves, vector, got, p_high, p_low, prior, order_row)


def put_halves(core, keep, give, at, first, second):
    even = core[0] == 0
    keep[pl.ds(at, 8), :] = jnp.where(even, first, second)
    give[pl.ds(at, 8), :] = jnp.where(even, second, first)


def unfold_first_kernel(core, field, p_high, p_low, keep, give):
    def put(at, value):
        put_halves(core, keep, give, at, value[0:8] * INV, value[8:16] * INV)

    by_slot(field, p_high, p_low, DEG_PAD, NT, put)


def unfold_second_kernel(core, seen, p_high, p_low, keep, give, rows):
    t = OWN_TILES
    rows[...] = jnp.concatenate([seen[g, 0:t, :] for g in range(GROUPS)], 0).T
    energy = source_sum(seen, t)
    lane = lax.broadcasted_iota(jnp.int32, (8, DEG_PAD), 1)

    def put(at, value):
        first = jnp.where(lane == DEGREES, energy, value[0:8] * (INV * INV))
        put_halves(core, keep, give, at, first, value[8:16] * (INV * INV))

    by_slot(rows, p_high, p_low, DEG_PAD, NT, put)


def unfold(core, field, p_high, p_low, second):
    half = jax.ShapeDtypeStruct((SLOTS, DEG_PAD), F32)
    return pl.pallas_call(
        unfold_second_kernel if second else unfold_first_kernel,
        out_shape=[half, half],
        in_specs=[SMEM] + vmem(3),
        out_specs=vmem(2),
        scratch_shapes=[pltpu.VMEM((LANES, TILES), F32)] if second else [],
        compiler_params=params(8),
        cost_estimate=cost(64 * SLOTS * DEG_PAD * TILES, 4 * SLOTS * DEG_PAD * TILES),
    )(core, field, p_high, p_low)


def slot_hits(order_row):
    wanted = lax.broadcasted_iota(jnp.int32, (ORDERS, LANES), 0).astype(F32)
    return jnp.where(wanted == order_row, 1.0, 0.0).astype(BF)


def two_halves(x):
    lane = lax.broadcasted_iota(jnp.int32, x.shape, 1)
    return jnp.where(lane < SLOTS, x, 0.0), jnp.where((lane >= SLOTS) & (lane < 2 * SLOTS), x, 0.0)


def to_natural(pieces, hits):
    total = None
    for per_source, hit in zip(pieces, hits):
        rows = [half for x in per_source for half in two_halves(x)]
        high, low = split(jnp.concatenate(rows, 0))
        got = dot(jnp.concatenate([high, low], 0), hit, NT)
        total = got if total is None else total + got
    n = total.shape[0] // 2
    return total[:n] + total[n:]


def own_tiles(me, z_high, z_low):
    shape = (OWN_TILES, TILES)
    wanted = lax.broadcasted_iota(jnp.int32, shape, 0) + me[0] * OWN_TILES
    pick = jnp.where(lax.broadcasted_iota(jnp.int32, shape, 1) == wanted, 1.0, 0.0).astype(BF)
    return [
        dot(pick, z_high[pl.ds(c * ORDERS, ORDERS), :], NT) + dot(pick, z_low[pl.ds(c * ORDERS, ORDERS), :], NT)
        for c in range(2)
    ]


def wave_parts(wave):
    return [wave.at[pl.ds(i * ORDERS, ORDERS), :] for i in range(4)]


def grid_first_kernel(me, got, z_high, z_low, wave, back, kept):
    c1, c1l, s1, s1l = wave_parts(wave)
    t = OWN_TILES
    hits = [slot_hits(got[g, EXTRA_FIRST : EXTRA_FIRST + 1, 0:LANES]) for g in range(GROUPS)]
    nat = to_natural(
        [
            [got[g, F_ROWS:EXTRA_FIRST, 0:LANES], got[g, F_ROWS:EXTRA_FIRST, LANES:TILES]]
            for g in range(GROUPS)
        ],
        hits,
    )
    own_c, own_s = own_tiles(me, z_high, z_low)
    k = lax.broadcasted_iota(jnp.int32, (1, ORDERS), 1)
    k_first = jnp.where(k == 0, 1.0 / GRID, 2.0 / GRID)
    k_second = jnp.where(k + ORDERS <= 2 * (DEGREES - 1), 2.0 / GRID, 0.0)
    near_c, near_s = nat[0:t] * k_first, nat[t : 2 * t] * k_first
    far_c, far_s = nat[2 * t : 3 * t] * k_second, nat[3 * t :] * k_second
    by_c = mm3(jnp.concatenate([own_c, near_c, far_c, far_s], 0), c1[...], c1l[...], NN)
    by_s = mm3(jnp.concatenate([own_s, near_s, far_c, far_s], 0), s1[...], s1l[...], NN)
    q = lax.broadcasted_iota(jnp.int32, (1, HALF), 1) % 4
    root = math.sqrt(0.5)
    turn_c = jnp.where((q == 0) | (q == 3), root, -root)
    turn_s = jnp.where(q < 2, root, -root)
    even, odd = by_c[:t], by_s[:t]
    w_even = by_c[t : 2 * t] + turn_c * by_c[2 * t : 3 * t] - turn_s * by_s[2 * t : 3 * t]
    w_odd = by_s[t : 2 * t] + turn_c * by_s[3 * t :] + turn_s * by_c[3 * t :]
    h_even = 2.0 * (w_even * even + w_odd * odd)
    h_odd = 2.0 * (w_even * odd + w_odd * even)
    energy = all_sum(h_even * even + h_odd * odd)
    kept[0] = even
    kept[1] = odd
    kept[2] = w_even
    kept[3] = w_odd
    hc = mm3(h_even, c1[...], c1l[...], NT)
    hs = mm3(h_odd, s1[...], s1l[...], NT)
    c_high, c_low = split(hc)
    s_high, s_low = split(hs)
    stack = jnp.concatenate([c_high, c_low, s_high, s_low], 0)
    lane = lax.broadcasted_iota(jnp.int32, (t, LANES), 1)
    for g in range(GROUPS):
        slots = dot(stack, hits[g], NN)
        back[g, 0:t, :] = jnp.where(
            lane < SLOTS, slots[0:t] + slots[t : 2 * t], slots[2 * t : 3 * t] + slots[3 * t :]
        )
        back[g, t : t + 8, :] = jnp.broadcast_to(energy, (8, LANES))


def grid_first(me, got, tables, waves):
    return pl.pallas_call(
        grid_first_kernel,
        out_shape=[
            jax.ShapeDtypeStruct((GROUPS, OWN_TILES + 8, LANES), F32),
            jax.ShapeDtypeStruct((4, OWN_TILES, HALF), F32),
        ],
        in_specs=[SMEM] + vmem(4),
        out_specs=vmem(2),
        compiler_params=params(8),
        cost_estimate=cost(10**9, 5 * 10**6),
    )(me, got, *tables, waves)


def grid_second_kernel(me, step, got, z_high, z_low, kept, wave, out):
    c1, c1l, s1, s1l = wave_parts(wave)
    own_c, own_s = own_tiles(me, z_high, z_low)
    ratio = source_sum(got, EXTRA_SECOND + 1) / step[1:2, 0:1]
    even = mm3(own_c, c1[...], c1l[...], NN) + ratio * kept[0]
    odd = mm3(own_s, s1[...], s1l[...], NN) + ratio * kept[1]
    w_even, w_odd = kept[2], kept[3]
    terms = 2.0 * w_even * (even * even + odd * odd) + 4.0 * w_odd * (even * odd)
    energy = all_sum(terms)
    out[...] = jnp.broadcast_to(energy, (8, LANES))


def grid_second(me, step, got, tables, kept, waves):
    return pl.pallas_call(
        grid_second_kernel,
        out_shape=jax.ShapeDtypeStruct((8, LANES), F32),
        in_specs=[SMEM] + vmem(6),
        out_specs=pl.BlockSpec(memory_space=pltpu.VMEM),
        compiler_params=params(8),
        cost_estimate=cost(10**9, 5 * 10**6),
    )(me, step, got, *tables, kept, waves)


S_WIDTH = 512


def lookup_kernel(extra_row, got, z_high, z_low):
    lane = lax.broadcasted_iota(jnp.int32, (1, LANES), 1)
    blank = jnp.zeros((LANES - F_ROWS, TILES), F32)
    high, low = split(
        jnp.concatenate([x for g in range(GROUPS) for x in (got[g, 0:F_ROWS, :], blank)], 0)
    )
    order_rows = [got[g, extra_row : extra_row + 1, 0:LANES] for g in range(GROUPS)]
    for c in range(2):
        ours = (lane >= c * SLOTS) & (lane < (c + 1) * SLOTS)
        hits = jnp.concatenate([slot_hits(jnp.where(ours, row, -1.0)) for row in order_rows], 1)
        z_high[pl.ds(c * ORDERS, ORDERS), :] = dot(hits, high, NN).astype(BF)
        z_low[pl.ds(c * ORDERS, ORDERS), :] = dot(hits, low, NN).astype(BF)


def lookup(got, extra_row):
    shape = jax.ShapeDtypeStruct((2 * ORDERS, TILES), BF)
    return pl.pallas_call(
        lambda *refs: lookup_kernel(extra_row, *refs),
        out_shape=[shape, shape],
        in_specs=vmem(1),
        out_specs=vmem(2),
        compiler_params=params(10),
        cost_estimate=cost(10**9, 3 * 10**6),
    )(got)


def values_kernel(start, me, gate, high_r, low_r, tile_r, z_high, z_low, out):
    first = (me[0] + gate[0]) * (high_r.shape[1] // GROUPS) + start * S_WIDTH
    near_order = lax.broadcasted_iota(jnp.int32, (8, S_WIDTH), 0).astype(F32)

    def step(i, carry):
        at = pl.ds(pl.multiple_of(first + i * S_WIDTH, S_WIDTH), S_WIDTH)
        hits_here = tile_hits(tile_r[:, at], S_WIDTH)
        picked = dot(z_high[...], hits_here, NN) + dot(z_low[...], hits_here, NN)
        high, low = high_r[:, at], low_r[:, at]
        c, s = turn_trig(near_order, high, low)
        c8, s8 = turn_trig(8.0, high, low)
        c8 = jnp.broadcast_to(c8, c.shape)
        s8 = jnp.broadcast_to(s8, c.shape)
        total = None
        for b in range(ORDERS // 8):
            add = c * picked[8 * b : 8 * b + 8, :] + s * picked[ORDERS + 8 * b : ORDERS + 8 * b + 8, :]
            total = add if total is None else total + add
            c, s = c * c8 - s * s8, s * c8 + c * s8
        row = jnp.sum(total, axis=0, keepdims=True)
        for j in range(S_WIDTH // LANES):
            out[pl.ds(i * (S_WIDTH // LANES) + j, 1), :] = row[:, j * LANES : (j + 1) * LANES]
        return carry

    lax.fori_loop(0, out.shape[0] * LANES // S_WIDTH, step, 0)


def point_values(me, points, tables, start, rows, gate):
    high, low, tile = points
    return pl.pallas_call(
        lambda *refs: values_kernel(start, *refs),
        out_shape=jax.ShapeDtypeStruct((rows * S_WIDTH // LANES, LANES), F32),
        in_specs=[SMEM, SMEM] + vmem(5),
        out_specs=pl.BlockSpec(memory_space=pltpu.VMEM),
        compiler_params=params(10),
        cost_estimate=cost(8 * ORDERS * TILES * rows * S_WIDTH, 10**6),
    )(me, gate, high, low, tile, *tables)


def final_kernel(last, step, got, vector, next_vector, observed, fitted, coefficients):
    rows = fitted.shape[1]
    alpha, norm, prior_00 = step[0:1, 0:1], step[1:2, 0:1], step[2:3, 0:1]
    norm_1 = source_sum(got, EXTRA_SECOND + 1)
    prior_01 = source_sum(got, EXTRA_SECOND + 2)
    prior_11 = source_sum(got, EXTRA_SECOND + 3)
    energy = source_sum(last, 2 * rows)
    ratio = norm_1 / norm
    curvature = energy * (INV * INV) + prior_11 + 2.0 * ratio * prior_01 + ratio * ratio * prior_00
    beta = norm_1 / curvature
    on_first = alpha + beta * ratio
    coefficients[...] = on_first * vector[...] + beta * next_vector[...]
    on_first, beta = on_first * INV, beta * INV
    for g in range(GROUPS):
        fitted[g] = observed[g] - (on_first * last[g, 0:rows, :] + beta * last[g, rows : 2 * rows, :])


def final(last, step, got, vector, next_vector, observed):
    return pl.pallas_call(
        final_kernel,
        out_shape=[
            jax.ShapeDtypeStruct(observed.shape, F32),
            jax.ShapeDtypeStruct(vector.shape, F32),
        ],
        in_specs=vmem(6),
        out_specs=vmem(2),
        compiler_params=params(8),
        cost_estimate=cost(10**7, 3 * 10**6),
    )(last, step, got, vector, next_vector, observed)


def waves():
    k = np.arange(ORDERS)[:, None]
    q = np.arange(HALF)[None, :] * 2 + 1
    phase = 2 * np.pi * ((k * q) % (2 * GRID)) / (2 * GRID)
    out = []
    for f in (np.cos(phase), np.sin(phase)):
        high = f.astype(jnp.bfloat16)
        out += [high, (f - high.astype(np.float64)).astype(jnp.bfloat16)]
    return np.concatenate(out, 0)


def sectoral_values(orders, sines):
    single = (orders == 0.0).astype(F32)
    log_lead = 0.5 * (
        jnp.log(2.0 - single)
        + lax.lgamma(orders + 1.5)
        - lax.lgamma(orders * 0.0 + 1.5)
        - lax.lgamma(orders + 1.0)
    )
    return jnp.exp(log_lead + orders * jnp.log(sines))


def exchange(x, d):
    return lax.ppermute(x, "pts", [(i, i ^ d) for i in range(16)])


def gated(x, move, task):
    if task is None:
        return move(x), None
    x, gate = lax.optimization_barrier((x, jnp.zeros((1,), jnp.int32)))
    return lax.optimization_barrier((move(x), task(gate)))


def halves_total(keep, give, tasks=(None, None)):
    x = keep + exchange(give, 1)
    (x, across, near, both), first = gated(
        x, lambda v: (v, exchange(v, 4), exchange(v, 2), exchange(v, 6)), tasks[0]
    )
    x = (x + across) + (near + both)
    (x, far), second = gated(x, lambda v: (v, exchange(v, 8)), tasks[1])
    x = x + far
    return (x, exchange(x, 1)), [first, second]


def pts_total(x, tasks):
    made = []
    for d, task in zip((1, 2, 4, 8), tasks):
        (x, other), out = gated(x, lambda v: (v, exchange(v, d)), task)
        x = x + other
        made.append(out)
    return x, [m for m in made if m is not None]


def swap(x):
    return lax.all_to_all(x, "coef", 0, 0)


def shards(colatitude, longitude, tile_of_point, order_of_slot, observations, obs_weight, prior):
    me = lax.axis_index("coef").astype(jnp.int32).reshape(1)
    place = lax.axis_index("pts").astype(jnp.int32)
    core = (place & 1).reshape(1)
    me, core, place, order_of_slot, longitude, tile_of_point = lax.optimization_barrier(
        (me, core, place * TILES, order_of_slot, longitude, tile_of_point)
    )
    local_tile = (tile_of_point - place).astype(F32)
    order = order_of_slot.astype(F32)
    orders = jnp.broadcast_to(order[:, None], (SLOTS, LANES))
    cosine = jnp.cos(colatitude)[None, :]
    sectoral = sectoral_values(order[:, None], jnp.sin(colatitude)[None, :])
    degree = np.arange(DEG_PAD, dtype=np.float64)
    scale = jnp.asarray((1.0 / (4 * degree * degree - 1)).astype(np.float32))
    wave = jnp.asarray(waves())

    turn = 2.0 * math.pi
    turn_high = 6.28125
    turn_low = turn - turn_high
    high = jnp.round(longitude * (4096.0 / turn)) * (1.0 / 4096.0)
    low = ((longitude - high * turn_high) - high * turn_low) * (1.0 / turn)
    far = high * ORDERS
    far = ((far - jnp.round(far)) + low * ORDERS) * turn
    weighted = obs_weight * observations
    points = [x[None] for x in (high, low, obs_weight, weighted, jnp.cos(far), jnp.sin(far), local_tile)]
    near = points[0], points[1], points[6]

    field, w_first, w_second = moments(points, orders)
    p_high, p_low = legendre_table(orders, cosine, sectoral, scale)
    prior_row = jnp.pad(prior, (0, DEG_PAD - DEGREES))[None, :]
    order_row = jnp.concatenate([order, order, jnp.full((LANES - 2 * SLOTS,), -1.0, F32)])[None]
    own_rows = high.shape[0] // (GROUPS * S_WIDTH)
    half = own_rows // 2

    halves, _ = halves_total(*unfold(core, field, p_high, p_low, False))
    sent, residual = fold_first(core, halves, p_high, p_low, prior_row, order_row, w_first, w_second)
    sent, me, core = lax.optimization_barrier((sent, me, core))
    got, me, core = lax.optimization_barrier((swap(sent), me, core))

    tables_0 = lookup(got, EXTRA_FIRST)
    back, kept = grid_first(me, got, tables_0, wave)
    held = (me, core, tables_0, kept, near)
    back, held = lax.optimization_barrier((back, held))
    seen, (me, core, tables_0, kept, near) = lax.optimization_barrier((swap(back), held))
    halves, values_0 = halves_total(
        *unfold(core, seen, p_high, p_low, True),
        [
            lambda gate: point_values(me, near, tables_0, 0, half, gate),
            lambda gate: point_values(me, near, tables_0, half, own_rows - half, gate),
        ],
    )
    sent_1, residual_1, step = fold_second(core, halves, residual, got, p_high, p_low, prior_row, order_row)
    held = (me, values_0, kept, near, residual, residual_1, step)
    sent_1, held = lax.optimization_barrier((sent_1, held))
    got_1, held = lax.optimization_barrier((swap(sent_1), held))
    me, values_0, kept, near, residual, residual_1, step = held
    tables_1 = lookup(got_1, EXTRA_SECOND)
    part = grid_second(me, step, got_1, tables_1, kept, wave)
    energy_1, values_1 = pts_total(
        part,
        [
            None,
            lambda gate: point_values(me, near, tables_1, 0, half, gate),
            lambda gate: point_values(me, near, tables_1, half, own_rows - half, gate),
            None,
        ],
    )
    payload = jnp.concatenate(
        values_0 + values_1 + [energy_1], 0
    )
    last = swap(jnp.broadcast_to(payload[None], (GROUPS,) + payload.shape))
    residual_out, vector = final(
        last, step, got_1, residual, residual_1, observations.reshape(GROUPS, -1, LANES)
    )
    coefficients = vector.reshape(2, SLOTS, DEG_PAD)[:, :, :DEGREES].transpose(2, 0, 1)
    return coefficients, residual_out.reshape(-1)


def solution(mesh):
    placed = (P("pts"), P("pts"), P("pts"), P("coef"), P("pts"), P("pts"), P())
    return jax.shard_map(
        shards,
        mesh=mesh,
        in_specs=placed,
        out_specs=(P(None, None, "coef"), P("pts")),
        check_vma=False,
    )
```

```python
import math
import numpy as np
import jax
import jax.numpy as jnp
from jax import lax
from jax.experimental import pallas as pl
from jax.experimental.pallas import tpu as pltpu
from jax.sharding import PartitionSpec as P

DEGREES = 301
DEG_PAD = 304
SLOTS = 40
TILES = 256
GROUPS = 8
OWN_TILES = TILES // GROUPS
ORDERS = 320
GRID = 1280
HALF = GRID // 2
LANES = 128
INV = 1.0 / DEGREES
BF = jnp.bfloat16
F32 = jnp.float32
ROUNDER = 12582912.0

NN = (((1,), (0,)), ((), ()))
NT = (((1,), (1,)), ((), ()))


def fit_even(f, terms):
    r = 0.502 * np.cos((np.arange(400) + 0.5) * np.pi / 800)
    a = np.stack([r ** (2 * k) for k in range(terms)], 1)
    return [float(v) for v in np.linalg.lstsq(a, f(r), rcond=None)[0]]


SIN_TERMS = fit_even(lambda r: np.sin(np.pi * r) / r, 5)
COS_TERMS = fit_even(lambda r: np.cos(np.pi * r), 5)


def horner(x, terms):
    total = terms[-1] * x + terms[-2]
    for term in terms[-3::-1]:
        total = total * x + term
    return total


def turn_trig(order, high, low):
    whole = order * high
    near = (whole + ROUNDER) - ROUNDER
    part = (whole - near) + order * low
    square = part * part
    s = horner(square, SIN_TERMS) * part
    c = horner(square, COS_TERMS)
    twice = s + s
    return 1.0 - twice * s, twice * c


def split(x):
    high = x.astype(BF)
    return high, (x - high.astype(F32)).astype(BF)


def dot(a, b, dims):
    return lax.dot_general(a, b, dims, preferred_element_type=F32)


def mm3(x, b_high, b_low, dims):
    rows = x.shape[0]
    high, low = split(x)
    both = dot(jnp.concatenate([high, low], 0), b_high, dims)
    return both[:rows] + both[rows:] + dot(high, b_low, dims)


def vmem(n):
    return [pl.BlockSpec(memory_space=pltpu.VMEM)] * n


SMEM = pl.BlockSpec(memory_space=pltpu.SMEM)


def params(mib):
    return pltpu.CompilerParams(vmem_limit_bytes=mib * 2**20)


def cost(flops, bytes_accessed):
    return pl.CostEstimate(flops=flops, bytes_accessed=bytes_accessed, transcendentals=0)


def tile_hits(tile_row, width):
    ids = lax.broadcasted_iota(jnp.int32, (TILES, width), 0).astype(F32)
    return jnp.where(ids == tile_row, 1.0, 0.0).astype(BF)


WIDTH = 2048
UNROLL = 4


def moments_kernel(high_r, low_r, weight_r, value_r, c_far_r, s_far_r, tile_r, orders, field, w_first, w_second, total):
    total[...] = jnp.zeros_like(total)
    order = orders[...]

    def make(first):
        parts = []
        for j in range(WIDTH // LANES):
            at = pl.ds(pl.multiple_of(first + j * LANES, LANES), LANES)
            c, s = turn_trig(order, high_r[:, at], low_r[:, at])
            weight, value = weight_r[:, at], value_r[:, at]
            c_far, s_far = c_far_r[:, at], s_far_r[:, at]
            wc, ws = weight * c, weight * s
            rows = jnp.concatenate(
                [value * c, value * s, wc, ws, wc * c_far - ws * s_far, ws * c_far + wc * s_far], 0
            )
            parts.append(split(rows) + (tile_hits(tile_r[:, at], LANES),))
        high, low, hits = [jnp.concatenate(x, 1) for x in zip(*parts)]
        return jnp.concatenate([high, low], 0), hits

    def step(i, carry):
        add = None
        for part in range(UNROLL):
            rows, hits = make((i * UNROLL + part) * WIDTH)
            got = dot(rows, hits, NT)
            add = got if add is None else add + got
        total[...] += add
        return carry

    lax.fori_loop(0, high_r.shape[1] // (WIDTH * UNROLL), step, 0)
    whole = total[0 : 6 * SLOTS] + total[6 * SLOTS : 12 * SLOTS]
    field[...] = whole[0 : 2 * SLOTS]
    blank = jnp.zeros((LANES - 2 * SLOTS, TILES), F32)
    w_first[...] = jnp.concatenate([whole[2 * SLOTS : 4 * SLOTS], blank], 0).T
    w_second[...] = jnp.concatenate([whole[4 * SLOTS : 6 * SLOTS], blank], 0).T


def moments(points, orders):
    n = points[0].shape[1]
    return pl.pallas_call(
        moments_kernel,
        out_shape=[
            jax.ShapeDtypeStruct((2 * SLOTS, TILES), F32),
            jax.ShapeDtypeStruct((TILES, LANES), F32),
            jax.ShapeDtypeStruct((TILES, LANES), F32),
        ],
        in_specs=vmem(8),
        out_specs=vmem(3),
        scratch_shapes=[pltpu.VMEM((12 * SLOTS, TILES), F32)],
        compiler_params=params(12),
        cost_estimate=cost(2 * 12 * SLOTS * TILES * n, 32 * n),
    )(*points, orders)


def table_kernel(orders, cosine, sectoral, scale, p_high, p_low, left, right):
    order = jnp.broadcast_to(orders[:, 0:1], (SLOTS, TILES))
    order_sq = orders[...] * orders[...]
    cos_row = jnp.broadcast_to(cosine[...], (SLOTS, TILES))
    start = sectoral[...]

    def put(n, value):
        for b in range(SLOTS // 8):
            at = pl.ds(b * 8 * DEG_PAD + n, 8, stride=DEG_PAD)
            left[at, :] = value[8 * b : 8 * b + 8, 0:LANES]
            right[at, :] = value[8 * b : 8 * b + 8, LANES:TILES]

    def step(n, carried):
        recent, earlier, back = carried
        degree = n.astype(F32)
        ratio = jnp.maximum((degree * degree - order_sq) * scale[n], 1e-20)
        up = lax.rsqrt(ratio)
        this_back = ratio * up
        up2 = jnp.concatenate([up, up], 1)
        back2 = jnp.concatenate([back, back], 1)
        grown = up2 * (cos_row * recent - back2 * earlier)
        value = jnp.where(order > degree, 0.0, jnp.where(order == degree, start, grown))
        put(n, value)
        return value, recent, this_back

    empty = jnp.zeros((SLOTS, TILES), F32)
    unset = start * 0.0
    lax.fori_loop(0, DEG_PAD, step, (unset, unset, order_sq * 0.0), unroll=4)
    for n in range(DEGREES, DEG_PAD):
        put(n, empty)

    def pack(slot, carry):
        at = pl.ds(pl.multiple_of(slot * DEG_PAD, 8), DEG_PAD)
        high, low = split(jnp.concatenate([left[at, :], right[at, :]], 1))
        p_high[slot] = high
        p_low[slot] = low
        return carry

    lax.fori_loop(0, SLOTS, pack, 0)


def legendre_table(orders, cosine, sectoral, scale):
    shape = jax.ShapeDtypeStruct((SLOTS, DEG_PAD, TILES), BF)
    return pl.pallas_call(
        table_kernel,
        out_shape=[shape, shape],
        in_specs=vmem(3) + [SMEM],
        out_specs=vmem(2),
        scratch_shapes=[pltpu.VMEM((SLOTS * DEG_PAD, LANES), F32)] * 2,
        compiler_params=params(30),
        cost_estimate=cost(20 * SLOTS * DEG_PAD * TILES, 4 * SLOTS * DEG_PAD * TILES),
    )(orders, cosine, sectoral, scale)


def slot_group(vector, at, high_of, low_of, width, dims):
    row = lax.broadcasted_iota(jnp.int32, (16, width), 0)
    rows = jnp.concatenate([vector[pl.ds(at, 8), :], vector[pl.ds(at + SLOTS, 8), :]], 0)
    high, low = split(rows)
    both = jnp.concatenate([high, low], 0)
    out = jnp.zeros((16, width), F32)
    for i in range(8):
        first = dot(both, high_of(at + i), dims)
        total = first[0:16] + first[16:32] + dot(high, low_of(at + i), dims)
        out = jnp.where((row == i) | (row == i + 8), total, out)
    return out


def by_slot(vector, p_high, p_low, width, dims, put, ready=None):
    def group(g, carry):
        at = pl.multiple_of(g * 8, 8)
        if ready is not None:
            ready(g)
        put(at, slot_group(vector, at, lambda i: p_high[i], lambda i: p_low[i], width, dims))
        return carry

    lax.fori_loop(0, SLOTS // 8, group, 0)


F_ROWS = 2 * SLOTS
EXTRA_FIRST = F_ROWS + OWN_TILES
EXTRA_SECOND = F_ROWS


def all_sum(x):
    return jnp.sum(jnp.sum(x, axis=1, keepdims=True), axis=0, keepdims=True)


def extra_rows(order_row, sums):
    rows = [order_row] + [jnp.broadcast_to(x, (1, LANES)) for x in sums]
    rows = jnp.concatenate(rows + [jnp.zeros((8 - len(rows), LANES), F32)], 0)
    return jnp.concatenate([rows, rows], 1)


def source_sum(got, row):
    total = got[0, row : row + 1, 0:1]
    for g in range(1, GROUPS):
        total = total + got[g, row : row + 1, 0:1]
    return total


def fold_into(vector, p_high, p_low, rows):
    def put(at, value):
        rows[pl.ds(at, 8), :] = value[0:8]
        rows[pl.ds(at + SLOTS, 8), :] = value[8:16]

    by_slot(vector, p_high, p_low, TILES, NN, put)
    return rows[...]


def join(core, mine, other):
    even = core[0] == 0
    mine, other = mine[...], other[...]
    return jnp.concatenate([jnp.where(even, mine, other), jnp.where(even, other, mine)], 0)


def fold_first_kernel(core, mine, other, p_high, p_low, prior, order_row, w_first, w_second, sent, vector, rows):
    v = join(core, mine, other)
    vector[...] = v
    folded = fold_into(vector, p_high, p_low, rows)
    extra = extra_rows(order_row[...], [all_sum(v * v), all_sum(prior[...] * v * v)])
    t = OWN_TILES
    for g in range(GROUPS):
        sent[g, 0:F_ROWS, :] = folded
        sent[g, F_ROWS:EXTRA_FIRST, 0:LANES] = w_first[g * t : (g + 1) * t, :]
        sent[g, F_ROWS:EXTRA_FIRST, LANES:TILES] = w_second[g * t : (g + 1) * t, :]
        sent[g, EXTRA_FIRST : EXTRA_FIRST + 8, :] = extra


def fold_first(core, halves, p_high, p_low, prior, order_row, w_first, w_second):
    return pl.pallas_call(
        fold_first_kernel,
        out_shape=[
            jax.ShapeDtypeStruct((GROUPS, EXTRA_FIRST + 8, TILES), F32),
            jax.ShapeDtypeStruct((2 * SLOTS, DEG_PAD), F32),
        ],
        in_specs=[SMEM] + vmem(8),
        out_specs=vmem(2),
        scratch_shapes=[pltpu.VMEM((2 * SLOTS, TILES), F32)],
        compiler_params=params(20),
        cost_estimate=cost(64 * SLOTS * DEG_PAD * TILES, 4 * SLOTS * DEG_PAD * TILES),
    )(core, *halves, p_high, p_low, prior, order_row, w_first, w_second)


def fold_second_kernel(core, mine, other, vector, got, p_high, p_low, prior, order_row, sent, next_vector, step, rows):
    v = vector[...]
    applied = join(core, mine, other)
    lane = lax.broadcasted_iota(jnp.int32, v.shape, 1)
    norm = source_sum(got, EXTRA_FIRST + 1)
    weighed = source_sum(got, EXTRA_FIRST + 2)
    alpha = norm / (applied[0:1, DEGREES : DEGREES + 1] * (INV * INV) + weighed)
    r = v - alpha * jnp.where(lane < DEGREES, applied + prior[...] * v, 0.0)
    next_vector[...] = r
    step[...] = jnp.concatenate(
        [jnp.broadcast_to(x, (1, LANES)) for x in (alpha, norm, weighed)] + [jnp.zeros((5, LANES), F32)], 0
    )
    folded = fold_into(next_vector, p_high, p_low, rows)
    extra = extra_rows(
        order_row[...], [all_sum(r * r), all_sum(prior[...] * v * r), all_sum(prior[...] * r * r)]
    )
    for g in range(GROUPS):
        sent[g, 0:F_ROWS, :] = folded
        sent[g, EXTRA_SECOND : EXTRA_SECOND + 8, :] = extra


def fold_second(core, halves, vector, got, p_high, p_low, prior, order_row):
    return pl.pallas_call(
        fold_second_kernel,
        out_shape=[
            jax.ShapeDtypeStruct((GROUPS, EXTRA_SECOND + 8, TILES), F32),
            jax.ShapeDtypeStruct((2 * SLOTS, DEG_PAD), F32),
            jax.ShapeDtypeStruct((8, LANES), F32),
        ],
        in_specs=[SMEM] + vmem(8),
        out_specs=vmem(3),
        scratch_shapes=[pltpu.VMEM((2 * SLOTS, TILES), F32)],
        compiler_params=params(20),
        cost_estimate=cost(64 * SLOTS * DEG_PAD * TILES, 4 * SLOTS * DEG_PAD * TILES),
    )(core, *halves, vector, got, p_high, p_low, prior, order_row)


def put_halves(core, keep, give, at, first, second):
    even = core[0] == 0
    keep[pl.ds(at, 8), :] = jnp.where(even, first, second)
    give[pl.ds(at, 8), :] = jnp.where(even, second, first)


def unfold_first_kernel(core, field, p_high, p_low, keep, give):
    def put(at, value):
        put_halves(core, keep, give, at, value[0:8] * INV, value[8:16] * INV)

    by_slot(field, p_high, p_low, DEG_PAD, NT, put)


def unfold_second_kernel(core, seen, p_high, p_low, keep, give, rows):
    t = OWN_TILES
    rows[...] = jnp.concatenate([seen[g, 0:t, :] for g in range(GROUPS)], 0).T
    energy = source_sum(seen, t)
    lane = lax.broadcasted_iota(jnp.int32, (8, DEG_PAD), 1)

    def put(at, value):
        first = jnp.where(lane == DEGREES, energy, value[0:8] * (INV * INV))
        put_halves(core, keep, give, at, first, value[8:16] * (INV * INV))

    by_slot(rows, p_high, p_low, DEG_PAD, NT, put)


def unfold(core, field, p_high, p_low, second):
    half = jax.ShapeDtypeStruct((SLOTS, DEG_PAD), F32)
    return pl.pallas_call(
        unfold_second_kernel if second else unfold_first_kernel,
        out_shape=[half, half],
        in_specs=[SMEM] + vmem(3),
        out_specs=vmem(2),
        scratch_shapes=[pltpu.VMEM((LANES, TILES), F32)] if second else [],
        compiler_params=params(20),
        cost_estimate=cost(64 * SLOTS * DEG_PAD * TILES, 4 * SLOTS * DEG_PAD * TILES),
    )(core, field, p_high, p_low)


def slot_hits(order_row):
    wanted = lax.broadcasted_iota(jnp.int32, (ORDERS, LANES), 0).astype(F32)
    return jnp.where(wanted == order_row, 1.0, 0.0).astype(BF)


def two_halves(x):
    lane = lax.broadcasted_iota(jnp.int32, x.shape, 1)
    return jnp.where(lane < SLOTS, x, 0.0), jnp.where((lane >= SLOTS) & (lane < 2 * SLOTS), x, 0.0)


def to_natural(pieces, hits):
    total = None
    for per_source, hit in zip(pieces, hits):
        rows = [half for x in per_source for half in two_halves(x)]
        high, low = split(jnp.concatenate(rows, 0))
        got = dot(jnp.concatenate([high, low], 0), hit, NT)
        total = got if total is None else total + got
    n = total.shape[0] // 2
    return total[:n] + total[n:]


def own_tiles(me, z_high, z_low):
    shape = (OWN_TILES, TILES)
    wanted = lax.broadcasted_iota(jnp.int32, shape, 0) + me[0] * OWN_TILES
    pick = jnp.where(lax.broadcasted_iota(jnp.int32, shape, 1) == wanted, 1.0, 0.0).astype(BF)
    return [
        dot(pick, z_high[pl.ds(c * ORDERS, ORDERS), :], NT) + dot(pick, z_low[pl.ds(c * ORDERS, ORDERS), :], NT)
        for c in range(2)
    ]


def wave_parts(wave):
    return [wave.at[pl.ds(i * ORDERS, ORDERS), :] for i in range(4)]


def grid_first_kernel(me, got, z_high, z_low, wave, back, kept):
    c1, c1l, s1, s1l = wave_parts(wave)
    t = OWN_TILES
    hits = [slot_hits(got[g, EXTRA_FIRST : EXTRA_FIRST + 1, 0:LANES]) for g in range(GROUPS)]
    nat = to_natural(
        [
            [got[g, F_ROWS:EXTRA_FIRST, 0:LANES], got[g, F_ROWS:EXTRA_FIRST, LANES:TILES]]
            for g in range(GROUPS)
        ],
        hits,
    )
    own_c, own_s = own_tiles(me, z_high, z_low)
    k = lax.broadcasted_iota(jnp.int32, (1, ORDERS), 1)
    k_first = jnp.where(k == 0, 1.0 / GRID, 2.0 / GRID)
    k_second = jnp.where(k + ORDERS <= 2 * (DEGREES - 1), 2.0 / GRID, 0.0)
    near_c, near_s = nat[0:t] * k_first, nat[t : 2 * t] * k_first
    far_c, far_s = nat[2 * t : 3 * t] * k_second, nat[3 * t :] * k_second
    by_c = mm3(jnp.concatenate([own_c, near_c, far_c, far_s], 0), c1[...], c1l[...], NN)
    by_s = mm3(jnp.concatenate([own_s, near_s, far_c, far_s], 0), s1[...], s1l[...], NN)
    q = lax.broadcasted_iota(jnp.int32, (1, HALF), 1) % 4
    root = math.sqrt(0.5)
    turn_c = jnp.where((q == 0) | (q == 3), root, -root)
    turn_s = jnp.where(q < 2, root, -root)
    even, odd = by_c[:t], by_s[:t]
    w_even = by_c[t : 2 * t] + turn_c * by_c[2 * t : 3 * t] - turn_s * by_s[2 * t : 3 * t]
    w_odd = by_s[t : 2 * t] + turn_c * by_s[3 * t :] + turn_s * by_c[3 * t :]
    h_even = 2.0 * (w_even * even + w_odd * odd)
    h_odd = 2.0 * (w_even * odd + w_odd * even)
    energy = all_sum(h_even * even + h_odd * odd)
    kept[0] = even
    kept[1] = odd
    kept[2] = w_even
    kept[3] = w_odd
    hc = mm3(h_even, c1[...], c1l[...], NT)
    hs = mm3(h_odd, s1[...], s1l[...], NT)
    c_high, c_low = split(hc)
    s_high, s_low = split(hs)
    stack = jnp.concatenate([c_high, c_low, s_high, s_low], 0)
    lane = lax.broadcasted_iota(jnp.int32, (t, LANES), 1)
    for g in range(GROUPS):
        slots = dot(stack, hits[g], NN)
        back[g, 0:t, :] = jnp.where(
            lane < SLOTS, slots[0:t] + slots[t : 2 * t], slots[2 * t : 3 * t] + slots[3 * t :]
        )
        back[g, t : t + 8, :] = jnp.broadcast_to(energy, (8, LANES))


def grid_first(me, got, tables, waves):
    return pl.pallas_call(
        grid_first_kernel,
        out_shape=[
            jax.ShapeDtypeStruct((GROUPS, OWN_TILES + 8, LANES), F32),
            jax.ShapeDtypeStruct((4, OWN_TILES, HALF), F32),
        ],
        in_specs=[SMEM] + vmem(4),
        out_specs=vmem(2),
        compiler_params=params(8),
        cost_estimate=cost(10**9, 5 * 10**6),
    )(me, got, *tables, waves)


def grid_second_kernel(me, step, got, z_high, z_low, kept, wave, out):
    c1, c1l, s1, s1l = wave_parts(wave)
    own_c, own_s = own_tiles(me, z_high, z_low)
    ratio = source_sum(got, EXTRA_SECOND + 1) / step[1:2, 0:1]
    even = mm3(own_c, c1[...], c1l[...], NN) + ratio * kept[0]
    odd = mm3(own_s, s1[...], s1l[...], NN) + ratio * kept[1]
    w_even, w_odd = kept[2], kept[3]
    terms = 2.0 * w_even * (even * even + odd * odd) + 4.0 * w_odd * (even * odd)
    energy = all_sum(terms)
    out[...] = jnp.broadcast_to(energy, out.shape)


def grid_second(me, step, got, tables, kept, waves):
    return pl.pallas_call(
        grid_second_kernel,
        out_shape=jax.ShapeDtypeStruct((SLOTS, TILES), F32),
        in_specs=[SMEM] + vmem(6),
        out_specs=pl.BlockSpec(memory_space=pltpu.VMEM),
        compiler_params=params(8),
        cost_estimate=cost(10**9, 5 * 10**6),
    )(me, step, got, *tables, kept, waves)


S_WIDTH = 512


def lookup_kernel(extra_row, got, z_high, z_low):
    lane = lax.broadcasted_iota(jnp.int32, (1, LANES), 1)
    blank = jnp.zeros((LANES - F_ROWS, TILES), F32)
    high, low = split(
        jnp.concatenate([x for g in range(GROUPS) for x in (got[g, 0:F_ROWS, :], blank)], 0)
    )
    order_rows = [got[g, extra_row : extra_row + 1, 0:LANES] for g in range(GROUPS)]
    for c in range(2):
        ours = (lane >= c * SLOTS) & (lane < (c + 1) * SLOTS)
        hits = jnp.concatenate([slot_hits(jnp.where(ours, row, -1.0)) for row in order_rows], 1)
        z_high[pl.ds(c * ORDERS, ORDERS), :] = dot(hits, high, NN).astype(BF)
        z_low[pl.ds(c * ORDERS, ORDERS), :] = dot(hits, low, NN).astype(BF)


def lookup(got, extra_row):
    shape = jax.ShapeDtypeStruct((2 * ORDERS, TILES), BF)
    return pl.pallas_call(
        lambda *refs: lookup_kernel(extra_row, *refs),
        out_shape=[shape, shape],
        in_specs=vmem(1),
        out_specs=vmem(2),
        compiler_params=params(10),
        cost_estimate=cost(10**9, 3 * 10**6),
    )(got)


def values_kernel(start, me, gate, high_r, low_r, tile_r, z_high, z_low, out):
    first = (me[0] + gate[0]) * (high_r.shape[1] // GROUPS) + start * S_WIDTH
    near_order = lax.broadcasted_iota(jnp.int32, (8, S_WIDTH), 0).astype(F32)

    def step(i, carry):
        at = pl.ds(pl.multiple_of(first + i * S_WIDTH, S_WIDTH), S_WIDTH)
        hits_here = tile_hits(tile_r[:, at], S_WIDTH)
        picked = dot(z_high[...], hits_here, NN) + dot(z_low[...], hits_here, NN)
        high, low = high_r[:, at], low_r[:, at]
        c, s = turn_trig(near_order, high, low)
        c8, s8 = turn_trig(8.0, high, low)
        c8 = jnp.broadcast_to(c8, c.shape)
        s8 = jnp.broadcast_to(s8, c.shape)
        total = None
        for b in range(ORDERS // 8):
            add = c * picked[8 * b : 8 * b + 8, :] + s * picked[ORDERS + 8 * b : ORDERS + 8 * b + 8, :]
            total = add if total is None else total + add
            c, s = c * c8 - s * s8, s * c8 + c * s8
        row = jnp.sum(total, axis=0, keepdims=True)
        for j in range(S_WIDTH // LANES):
            out[pl.ds(i * (S_WIDTH // LANES) + j, 1), :] = row[:, j * LANES : (j + 1) * LANES]
        return carry

    lax.fori_loop(0, out.shape[0] * LANES // S_WIDTH, step, 0, unroll=2)


def point_values(me, points, tables, start, rows, gate):
    high, low, tile = points
    return pl.pallas_call(
        lambda *refs: values_kernel(start, *refs),
        out_shape=jax.ShapeDtypeStruct((rows * S_WIDTH // LANES, LANES), F32),
        in_specs=[SMEM, SMEM] + vmem(5),
        out_specs=pl.BlockSpec(memory_space=pltpu.VMEM),
        compiler_params=params(10),
        cost_estimate=cost(8 * ORDERS * TILES * rows * S_WIDTH, 10**6),
    )(me, gate, high, low, tile, *tables)


def final_kernel(last, step, got, vector, next_vector, observed, fitted, coefficients):
    rows = fitted.shape[1]
    alpha, norm, prior_00 = step[0:1, 0:1], step[1:2, 0:1], step[2:3, 0:1]
    norm_1 = source_sum(got, EXTRA_SECOND + 1)
    prior_01 = source_sum(got, EXTRA_SECOND + 2)
    prior_11 = source_sum(got, EXTRA_SECOND + 3)
    energy = source_sum(last, 2 * rows)
    ratio = norm_1 / norm
    curvature = energy * (INV * INV) + prior_11 + 2.0 * ratio * prior_01 + ratio * ratio * prior_00
    beta = norm_1 / curvature
    on_first = alpha + beta * ratio
    coefficients[...] = on_first * vector[...] + beta * next_vector[...]
    on_first, beta = on_first * INV, beta * INV
    for g in range(GROUPS):
        fitted[g] = observed[g] - (on_first * last[g, 0:rows, :] + beta * last[g, rows : 2 * rows, :])


def final(last, step, got, vector, next_vector, observed):
    return pl.pallas_call(
        final_kernel,
        out_shape=[
            jax.ShapeDtypeStruct(observed.shape, F32),
            jax.ShapeDtypeStruct(vector.shape, F32),
        ],
        in_specs=vmem(6),
        out_specs=vmem(2),
        compiler_params=params(8),
        cost_estimate=cost(10**7, 3 * 10**6),
    )(last, step, got, vector, next_vector, observed)


def waves():
    k = np.arange(ORDERS)[:, None]
    q = np.arange(HALF)[None, :] * 2 + 1
    phase = 2 * np.pi * ((k * q) % (2 * GRID)) / (2 * GRID)
    out = []
    for f in (np.cos(phase), np.sin(phase)):
        high = f.astype(jnp.bfloat16)
        out += [high, (f - high.astype(np.float64)).astype(jnp.bfloat16)]
    return np.concatenate(out, 0)


def sectoral_values(orders, sines):
    single = (orders == 0.0).astype(F32)
    log_lead = 0.5 * (
        jnp.log(2.0 - single)
        + lax.lgamma(orders + 1.5)
        - lax.lgamma(orders * 0.0 + 1.5)
        - lax.lgamma(orders + 1.0)
    )
    return jnp.exp(log_lead + orders * jnp.log(sines))


def exchange(x, d):
    return lax.ppermute(x, "pts", [(i, i ^ d) for i in range(16)])


def gated(x, move, task):
    if task is None:
        return move(x), None
    x, gate = lax.optimization_barrier((x, jnp.zeros((1,), jnp.int32)))
    return lax.optimization_barrier((move(x), task(gate)))


def chips_total(x, tasks):
    (x, across, near, both), first = gated(
        x, lambda v: (v, exchange(v, 4), exchange(v, 2), exchange(v, 6)), tasks[0]
    )
    x = (x + across) + (near + both)
    (x, far), second = gated(x, lambda v: (v, exchange(v, 8)), tasks[1])
    return x + far, [first, second]


def halves_total(keep, give, tasks=(None, None)):
    x, made = chips_total(keep + exchange(give, 1), tasks)
    return (x, exchange(x, 1)), made


def swap(x):
    return lax.all_to_all(x, "coef", 0, 0)


def shards(colatitude, longitude, tile_of_point, order_of_slot, observations, obs_weight, prior):
    me = lax.axis_index("coef").astype(jnp.int32).reshape(1)
    place = lax.axis_index("pts").astype(jnp.int32)
    core = (place & 1).reshape(1)
    me, core, place, order_of_slot, longitude, tile_of_point = lax.optimization_barrier(
        (me, core, place * TILES, order_of_slot, longitude, tile_of_point)
    )
    local_tile = (tile_of_point - place).astype(F32)
    order = order_of_slot.astype(F32)
    orders = jnp.broadcast_to(order[:, None], (SLOTS, LANES))
    cosine = jnp.cos(colatitude)[None, :]
    sectoral = sectoral_values(order[:, None], jnp.sin(colatitude)[None, :])
    degree = np.arange(DEG_PAD, dtype=np.float64)
    scale = jnp.asarray((1.0 / (4 * degree * degree - 1)).astype(np.float32))
    wave = jnp.asarray(waves())

    turn = 2.0 * math.pi
    turn_high = 6.28125
    turn_low = turn - turn_high
    high = jnp.round(longitude * (4096.0 / turn)) * (1.0 / 4096.0)
    low = ((longitude - high * turn_high) - high * turn_low) * (1.0 / turn)
    far = high * ORDERS
    far = ((far - jnp.round(far)) + low * ORDERS) * turn
    weighted = obs_weight * observations
    points = [x[None] for x in (high, low, obs_weight, weighted, jnp.cos(far), jnp.sin(far), local_tile)]
    near = points[0], points[1], points[6]

    field, w_first, w_second = moments(points, orders)
    p_high, p_low = legendre_table(orders, cosine, sectoral, scale)
    prior_row = jnp.pad(prior, (0, DEG_PAD - DEGREES))[None, :]
    order_row = jnp.concatenate([order, order, jnp.full((LANES - 2 * SLOTS,), -1.0, F32)])[None]
    own_rows = high.shape[0] // (GROUPS * S_WIDTH)
    half = own_rows // 2

    halves, _ = halves_total(*unfold(core, field, p_high, p_low, False))
    sent, residual = fold_first(core, halves, p_high, p_low, prior_row, order_row, w_first, w_second)
    sent, me, core = lax.optimization_barrier((sent, me, core))
    got, me, core = lax.optimization_barrier((swap(sent), me, core))

    tables_0 = lookup(got, EXTRA_FIRST)
    back, kept = grid_first(me, got, tables_0, wave)
    held = (me, core, tables_0, kept, near)
    back, held = lax.optimization_barrier((back, held))
    seen, (me, core, tables_0, kept, near) = lax.optimization_barrier((swap(back), held))
    halves, values_0 = halves_total(
        *unfold(core, seen, p_high, p_low, True),
        [
            lambda gate: point_values(me, near, tables_0, 0, half, gate),
            lambda gate: point_values(me, near, tables_0, half, own_rows - half, gate),
        ],
    )
    sent_1, residual_1, step = fold_second(core, halves, residual, got, p_high, p_low, prior_row, order_row)
    held = (me, values_0, kept, near, residual, residual_1, step)
    sent_1, held = lax.optimization_barrier((sent_1, held))
    got_1, held = lax.optimization_barrier((swap(sent_1), held))
    me, values_0, kept, near, residual, residual_1, step = held
    tables_1 = lookup(got_1, EXTRA_SECOND)
    part = grid_second(me, step, got_1, tables_1, kept, wave)
    energy_1, values_1 = chips_total(
        part + exchange(part, 1),
        [
            lambda gate: point_values(me, near, tables_1, 0, half, gate),
            lambda gate: point_values(me, near, tables_1, half, own_rows - half, gate),
        ],
    )
    payload = jnp.concatenate(
        values_0 + values_1 + [energy_1[0:8, 0:LANES]], 0
    )
    last = swap(jnp.broadcast_to(payload[None], (GROUPS,) + payload.shape))
    residual_out, vector = final(
        last, step, got_1, residual, residual_1, observations.reshape(GROUPS, -1, LANES)
    )
    coefficients = vector.reshape(2, SLOTS, DEG_PAD)[:, :, :DEGREES].transpose(2, 0, 1)
    return coefficients, residual_out.reshape(-1)


def solution(mesh):
    placed = (P("pts"), P("pts"), P("pts"), P("coef"), P("pts"), P("pts"), P())
    return jax.shard_map(
        shards,
        mesh=mesh,
        in_specs=placed,
        out_specs=(P(None, None, "coef"), P("pts")),
        check_vma=False,
    )
```

```python
import math
import numpy as np
import jax
import jax.numpy as jnp
from jax import lax
from jax.experimental import pallas as pl
from jax.experimental.pallas import tpu as pltpu
from jax.sharding import PartitionSpec as P

DEGREES = 301
DEG_PAD = 304
SLOTS = 40
TILES = 256
GROUPS = 8
OWN_TILES = TILES // GROUPS
ORDERS = 320
GRID = 1280
HALF = GRID // 2
LANES = 128
INV = 1.0 / DEGREES
BF = jnp.bfloat16
F32 = jnp.float32
ROUNDER = 12582912.0

NN = (((1,), (0,)), ((), ()))
NT = (((1,), (1,)), ((), ()))


def fit_even(f, terms):
    r = 0.502 * np.cos((np.arange(400) + 0.5) * np.pi / 800)
    a = np.stack([r ** (2 * k) for k in range(terms)], 1)
    return [float(v) for v in np.linalg.lstsq(a, f(r), rcond=None)[0]]


SIN_TERMS = fit_even(lambda r: np.sin(np.pi * r) / r, 5)
COS_TERMS = fit_even(lambda r: np.cos(np.pi * r), 5)


def horner(x, terms):
    total = terms[-1] * x + terms[-2]
    for term in terms[-3::-1]:
        total = total * x + term
    return total


def turn_trig(order, high, low):
    whole = order * high
    near = (whole + ROUNDER) - ROUNDER
    part = (whole - near) + order * low
    square = part * part
    s = horner(square, SIN_TERMS) * part
    c = horner(square, COS_TERMS)
    twice = s + s
    return 1.0 - twice * s, twice * c


def split(x):
    high = x.astype(BF)
    return high, (x - high.astype(F32)).astype(BF)


def dot(a, b, dims):
    return lax.dot_general(a, b, dims, preferred_element_type=F32)


def mm3(x, b_high, b_low, dims):
    rows = x.shape[0]
    high, low = split(x)
    both = dot(jnp.concatenate([high, low], 0), b_high, dims)
    return both[:rows] + both[rows:] + dot(high, b_low, dims)


def vmem(n):
    return [pl.BlockSpec(memory_space=pltpu.VMEM)] * n


SMEM = pl.BlockSpec(memory_space=pltpu.SMEM)


def params(mib):
    return pltpu.CompilerParams(vmem_limit_bytes=mib * 2**20)


def cost(flops, bytes_accessed):
    return pl.CostEstimate(flops=flops, bytes_accessed=bytes_accessed, transcendentals=0)


def tile_hits(tile_row, width):
    ids = lax.broadcasted_iota(jnp.int32, (TILES, width), 0).astype(F32)
    return jnp.where(ids == tile_row, 1.0, 0.0).astype(BF)


WIDTH = 2048
UNROLL = 4


def moments_kernel(high_r, low_r, weight_r, value_r, c_far_r, s_far_r, tile_r, orders, field, w_first, w_second, total):
    total[...] = jnp.zeros_like(total)
    order = orders[...]

    def make(first):
        parts = []
        for j in range(WIDTH // LANES):
            at = pl.ds(pl.multiple_of(first + j * LANES, LANES), LANES)
            c, s = turn_trig(order, high_r[:, at], low_r[:, at])
            weight, value = weight_r[:, at], value_r[:, at]
            c_far, s_far = c_far_r[:, at], s_far_r[:, at]
            wc, ws = weight * c, weight * s
            rows = jnp.concatenate(
                [value * c, value * s, wc, ws, wc * c_far - ws * s_far, ws * c_far + wc * s_far], 0
            )
            parts.append(split(rows) + (tile_hits(tile_r[:, at], LANES),))
        high, low, hits = [jnp.concatenate(x, 1) for x in zip(*parts)]
        return jnp.concatenate([high, low], 0), hits

    def step(i, carry):
        add = None
        for part in range(UNROLL):
            rows, hits = make((i * UNROLL + part) * WIDTH)
            got = dot(rows, hits, NT)
            add = got if add is None else add + got
        total[...] += add
        return carry

    lax.fori_loop(0, high_r.shape[1] // (WIDTH * UNROLL), step, 0)
    whole = total[0 : 6 * SLOTS] + total[6 * SLOTS : 12 * SLOTS]
    field[...] = whole[0 : 2 * SLOTS]
    blank = jnp.zeros((LANES - 2 * SLOTS, TILES), F32)
    w_first[...] = jnp.concatenate([whole[2 * SLOTS : 4 * SLOTS], blank], 0).T
    w_second[...] = jnp.concatenate([whole[4 * SLOTS : 6 * SLOTS], blank], 0).T


def moments(points, orders):
    n = points[0].shape[1]
    return pl.pallas_call(
        moments_kernel,
        out_shape=[
            jax.ShapeDtypeStruct((2 * SLOTS, TILES), F32),
            jax.ShapeDtypeStruct((TILES, LANES), F32),
            jax.ShapeDtypeStruct((TILES, LANES), F32),
        ],
        in_specs=vmem(8),
        out_specs=vmem(3),
        scratch_shapes=[pltpu.VMEM((12 * SLOTS, TILES), F32)],
        compiler_params=params(12),
        cost_estimate=cost(2 * 12 * SLOTS * TILES * n, 32 * n),
    )(*points, orders)


def table_kernel(orders, cosine, sectoral, scale, p_high, p_low, left, right):
    order = jnp.broadcast_to(orders[:, 0:1], (SLOTS, TILES))
    order_sq = orders[...] * orders[...]
    cos_row = jnp.broadcast_to(cosine[...], (SLOTS, TILES))
    start = sectoral[...]

    def put(n, value):
        for b in range(SLOTS // 8):
            at = pl.ds(b * 8 * DEG_PAD + n, 8, stride=DEG_PAD)
            left[at, :] = value[8 * b : 8 * b + 8, 0:LANES]
            right[at, :] = value[8 * b : 8 * b + 8, LANES:TILES]

    def step(n, carried):
        recent, earlier, back = carried
        degree = n.astype(F32)
        ratio = jnp.maximum((degree * degree - order_sq) * scale[n], 1e-20)
        up = lax.rsqrt(ratio)
        this_back = ratio * up
        up2 = jnp.concatenate([up, up], 1)
        back2 = jnp.concatenate([back, back], 1)
        grown = up2 * (cos_row * recent - back2 * earlier)
        value = jnp.where(order > degree, 0.0, jnp.where(order == degree, start, grown))
        put(n, value)
        return value, recent, this_back

    empty = jnp.zeros((SLOTS, TILES), F32)
    unset = start * 0.0
    lax.fori_loop(0, DEG_PAD, step, (unset, unset, order_sq * 0.0), unroll=8)
    for n in range(DEGREES, DEG_PAD):
        put(n, empty)

    def pack(slot, carry):
        at = pl.ds(pl.multiple_of(slot * DEG_PAD, 8), DEG_PAD)
        high, low = split(jnp.concatenate([left[at, :], right[at, :]], 1))
        p_high[slot] = high
        p_low[slot] = low
        return carry

    lax.fori_loop(0, SLOTS, pack, 0, unroll=4)


def legendre_table(orders, cosine, sectoral, scale):
    shape = jax.ShapeDtypeStruct((SLOTS, DEG_PAD, TILES), BF)
    return pl.pallas_call(
        table_kernel,
        out_shape=[shape, shape],
        in_specs=vmem(3) + [SMEM],
        out_specs=vmem(2),
        scratch_shapes=[pltpu.VMEM((SLOTS * DEG_PAD, LANES), F32)] * 2,
        compiler_params=params(30),
        cost_estimate=cost(20 * SLOTS * DEG_PAD * TILES, 4 * SLOTS * DEG_PAD * TILES),
    )(orders, cosine, sectoral, scale)


def slot_group(vector, at, high_of, low_of, width, dims):
    row = lax.broadcasted_iota(jnp.int32, (16, width), 0)
    rows = jnp.concatenate([vector[pl.ds(at, 8), :], vector[pl.ds(at + SLOTS, 8), :]], 0)
    high, low = split(rows)
    both = jnp.concatenate([high, low], 0)
    out = jnp.zeros((16, width), F32)
    for i in range(8):
        first = dot(both, high_of(at + i), dims)
        total = first[0:16] + first[16:32] + dot(high, low_of(at + i), dims)
        out = jnp.where((row == i) | (row == i + 8), total, out)
    return out


def by_slot(vector, p_high, p_low, width, dims, put, ready=None):
    def group(g, carry):
        at = pl.multiple_of(g * 8, 8)
        if ready is not None:
            ready(g)
        put(at, slot_group(vector, at, lambda i: p_high[i], lambda i: p_low[i], width, dims))
        return carry

    lax.fori_loop(0, SLOTS // 8, group, 0, unroll=True)


F_ROWS = 2 * SLOTS
EXTRA_FIRST = F_ROWS + OWN_TILES
EXTRA_SECOND = F_ROWS


def all_sum(x):
    return jnp.sum(jnp.sum(x, axis=1, keepdims=True), axis=0, keepdims=True)


def extra_rows(order_row, sums):
    rows = [order_row] + [jnp.broadcast_to(x, (1, LANES)) for x in sums]
    rows = jnp.concatenate(rows + [jnp.zeros((8 - len(rows), LANES), F32)], 0)
    return jnp.concatenate([rows, rows], 1)


def source_sum(got, row):
    total = got[0, row : row + 1, 0:1]
    for g in range(1, GROUPS):
        total = total + got[g, row : row + 1, 0:1]
    return total


def fold_into(vector, p_high, p_low, rows):
    def put(at, value):
        rows[pl.ds(at, 8), :] = value[0:8]
        rows[pl.ds(at + SLOTS, 8), :] = value[8:16]

    by_slot(vector, p_high, p_low, TILES, NN, put)
    return rows[...]


def join(core, mine, other):
    even = core[0] == 0
    mine, other = mine[...], other[...]
    return jnp.concatenate([jnp.where(even, mine, other), jnp.where(even, other, mine)], 0)


def fold_first_kernel(core, mine, other, p_high, p_low, prior, order_row, w_first, w_second, sent, vector, rows):
    v = join(core, mine, other)
    vector[...] = v
    folded = fold_into(vector, p_high, p_low, rows)
    extra = extra_rows(order_row[...], [all_sum(v * v), all_sum(prior[...] * v * v)])
    t = OWN_TILES
    for g in range(GROUPS):
        sent[g, 0:F_ROWS, :] = folded
        sent[g, F_ROWS:EXTRA_FIRST, 0:LANES] = w_first[g * t : (g + 1) * t, :]
        sent[g, F_ROWS:EXTRA_FIRST, LANES:TILES] = w_second[g * t : (g + 1) * t, :]
        sent[g, EXTRA_FIRST : EXTRA_FIRST + 8, :] = extra


def fold_first(core, halves, p_high, p_low, prior, order_row, w_first, w_second):
    return pl.pallas_call(
        fold_first_kernel,
        out_shape=[
            jax.ShapeDtypeStruct((GROUPS, EXTRA_FIRST + 8, TILES), F32),
            jax.ShapeDtypeStruct((2 * SLOTS, DEG_PAD), F32),
        ],
        in_specs=[SMEM] + vmem(8),
        out_specs=vmem(2),
        scratch_shapes=[pltpu.VMEM((2 * SLOTS, TILES), F32)],
        compiler_params=params(20),
        cost_estimate=cost(64 * SLOTS * DEG_PAD * TILES, 4 * SLOTS * DEG_PAD * TILES),
    )(core, *halves, p_high, p_low, prior, order_row, w_first, w_second)


def fold_second_kernel(core, mine, other, vector, got, p_high, p_low, prior, order_row, sent, next_vector, step, rows):
    v = vector[...]
    applied = join(core, mine, other)
    lane = lax.broadcasted_iota(jnp.int32, v.shape, 1)
    norm = source_sum(got, EXTRA_FIRST + 1)
    weighed = source_sum(got, EXTRA_FIRST + 2)
    alpha = norm / (applied[0:1, DEGREES : DEGREES + 1] * (INV * INV) + weighed)
    r = v - alpha * jnp.where(lane < DEGREES, applied + prior[...] * v, 0.0)
    next_vector[...] = r
    step[...] = jnp.concatenate(
        [jnp.broadcast_to(x, (1, LANES)) for x in (alpha, norm, weighed)] + [jnp.zeros((5, LANES), F32)], 0
    )
    folded = fold_into(next_vector, p_high, p_low, rows)
    extra = extra_rows(
        order_row[...], [all_sum(r * r), all_sum(prior[...] * v * r), all_sum(prior[...] * r * r)]
    )
    for g in range(GROUPS):
        sent[g, 0:F_ROWS, :] = folded
        sent[g, EXTRA_SECOND : EXTRA_SECOND + 8, :] = extra


def fold_second(core, halves, vector, got, p_high, p_low, prior, order_row):
    return pl.pallas_call(
        fold_second_kernel,
        out_shape=[
            jax.ShapeDtypeStruct((GROUPS, EXTRA_SECOND + 8, TILES), F32),
            jax.ShapeDtypeStruct((2 * SLOTS, DEG_PAD), F32),
            jax.ShapeDtypeStruct((8, LANES), F32),
        ],
        in_specs=[SMEM] + vmem(8),
        out_specs=vmem(3),
        scratch_shapes=[pltpu.VMEM((2 * SLOTS, TILES), F32)],
        compiler_params=params(20),
        cost_estimate=cost(64 * SLOTS * DEG_PAD * TILES, 4 * SLOTS * DEG_PAD * TILES),
    )(core, *halves, vector, got, p_high, p_low, prior, order_row)


def put_halves(core, keep, give, at, first, second):
    even = core[0] == 0
    keep[pl.ds(at, 8), :] = jnp.where(even, first, second)
    give[pl.ds(at, 8), :] = jnp.where(even, second, first)


def unfold_first_kernel(core, field, p_high, p_low, keep, give):
    def put(at, value):
        put_halves(core, keep, give, at, value[0:8] * INV, value[8:16] * INV)

    by_slot(field, p_high, p_low, DEG_PAD, NT, put)


def unfold_second_kernel(core, seen, p_high, p_low, keep, give, rows):
    t = OWN_TILES
    rows[...] = jnp.concatenate([seen[g, 0:t, :] for g in range(GROUPS)], 0).T
    energy = source_sum(seen, t)
    lane = lax.broadcasted_iota(jnp.int32, (8, DEG_PAD), 1)

    def put(at, value):
        first = jnp.where(lane == DEGREES, energy, value[0:8] * (INV * INV))
        put_halves(core, keep, give, at, first, value[8:16] * (INV * INV))

    by_slot(rows, p_high, p_low, DEG_PAD, NT, put)


def unfold(core, field, p_high, p_low, second):
    half = jax.ShapeDtypeStruct((SLOTS, DEG_PAD), F32)
    return pl.pallas_call(
        unfold_second_kernel if second else unfold_first_kernel,
        out_shape=[half, half],
        in_specs=[SMEM] + vmem(3),
        out_specs=vmem(2),
        scratch_shapes=[pltpu.VMEM((LANES, TILES), F32)] if second else [],
        compiler_params=params(20),
        cost_estimate=cost(64 * SLOTS * DEG_PAD * TILES, 4 * SLOTS * DEG_PAD * TILES),
    )(core, field, p_high, p_low)


def slot_hits(order_row):
    wanted = lax.broadcasted_iota(jnp.int32, (ORDERS, LANES), 0).astype(F32)
    return jnp.where(wanted == order_row, 1.0, 0.0).astype(BF)


def two_halves(x):
    lane = lax.broadcasted_iota(jnp.int32, x.shape, 1)
    return jnp.where(lane < SLOTS, x, 0.0), jnp.where((lane >= SLOTS) & (lane < 2 * SLOTS), x, 0.0)


def to_natural(pieces, hits):
    total = None
    for per_source, hit in zip(pieces, hits):
        rows = [half for x in per_source for half in two_halves(x)]
        high, low = split(jnp.concatenate(rows, 0))
        got = dot(jnp.concatenate([high, low], 0), hit, NT)
        total = got if total is None else total + got
    n = total.shape[0] // 2
    return total[:n] + total[n:]


def own_tiles(me, z_high, z_low):
    shape = (OWN_TILES, TILES)
    wanted = lax.broadcasted_iota(jnp.int32, shape, 0) + me[0] * OWN_TILES
    pick = jnp.where(lax.broadcasted_iota(jnp.int32, shape, 1) == wanted, 1.0, 0.0).astype(BF)
    return [
        dot(pick, z_high[pl.ds(c * ORDERS, ORDERS), :], NT) + dot(pick, z_low[pl.ds(c * ORDERS, ORDERS), :], NT)
        for c in range(2)
    ]


def wave_parts(wave):
    return [wave.at[pl.ds(i * ORDERS, ORDERS), :] for i in range(4)]


def grid_first_kernel(me, got, z_high, z_low, wave, back, kept):
    c1, c1l, s1, s1l = wave_parts(wave)
    t = OWN_TILES
    hits = [slot_hits(got[g, EXTRA_FIRST : EXTRA_FIRST + 1, 0:LANES]) for g in range(GROUPS)]
    nat = to_natural(
        [
            [got[g, F_ROWS:EXTRA_FIRST, 0:LANES], got[g, F_ROWS:EXTRA_FIRST, LANES:TILES]]
            for g in range(GROUPS)
        ],
        hits,
    )
    own_c, own_s = own_tiles(me, z_high, z_low)
    k = lax.broadcasted_iota(jnp.int32, (1, ORDERS), 1)
    k_first = jnp.where(k == 0, 1.0 / GRID, 2.0 / GRID)
    k_second = jnp.where(k + ORDERS <= 2 * (DEGREES - 1), 2.0 / GRID, 0.0)
    near_c, near_s = nat[0:t] * k_first, nat[t : 2 * t] * k_first
    far_c, far_s = nat[2 * t : 3 * t] * k_second, nat[3 * t :] * k_second
    by_c = mm3(jnp.concatenate([own_c, near_c, far_c, far_s], 0), c1[...], c1l[...], NN)
    by_s = mm3(jnp.concatenate([own_s, near_s, far_c, far_s], 0), s1[...], s1l[...], NN)
    q = lax.broadcasted_iota(jnp.int32, (1, HALF), 1) % 4
    root = math.sqrt(0.5)
    turn_c = jnp.where((q == 0) | (q == 3), root, -root)
    turn_s = jnp.where(q < 2, root, -root)
    even, odd = by_c[:t], by_s[:t]
    w_even = by_c[t : 2 * t] + turn_c * by_c[2 * t : 3 * t] - turn_s * by_s[2 * t : 3 * t]
    w_odd = by_s[t : 2 * t] + turn_c * by_s[3 * t :] + turn_s * by_c[3 * t :]
    h_even = 2.0 * (w_even * even + w_odd * odd)
    h_odd = 2.0 * (w_even * odd + w_odd * even)
    energy = all_sum(h_even * even + h_odd * odd)
    kept[0] = even
    kept[1] = odd
    kept[2] = w_even
    kept[3] = w_odd
    hc = mm3(h_even, c1[...], c1l[...], NT)
    hs = mm3(h_odd, s1[...], s1l[...], NT)
    c_high, c_low = split(hc)
    s_high, s_low = split(hs)
    stack = jnp.concatenate([c_high, c_low, s_high, s_low], 0)
    lane = lax.broadcasted_iota(jnp.int32, (t, LANES), 1)
    for g in range(GROUPS):
        slots = dot(stack, hits[g], NN)
        back[g, 0:t, :] = jnp.where(
            lane < SLOTS, slots[0:t] + slots[t : 2 * t], slots[2 * t : 3 * t] + slots[3 * t :]
        )
        back[g, t : t + 8, :] = jnp.broadcast_to(energy, (8, LANES))


def grid_first(me, got, tables, waves):
    return pl.pallas_call(
        grid_first_kernel,
        out_shape=[
            jax.ShapeDtypeStruct((GROUPS, OWN_TILES + 8, LANES), F32),
            jax.ShapeDtypeStruct((4, OWN_TILES, HALF), F32),
        ],
        in_specs=[SMEM] + vmem(4),
        out_specs=vmem(2),
        compiler_params=params(8),
        cost_estimate=cost(10**9, 5 * 10**6),
    )(me, got, *tables, waves)


def grid_second_kernel(me, step, got, z_high, z_low, kept, wave, out):
    c1, c1l, s1, s1l = wave_parts(wave)
    own_c, own_s = own_tiles(me, z_high, z_low)
    ratio = source_sum(got, EXTRA_SECOND + 1) / step[1:2, 0:1]
    even = mm3(own_c, c1[...], c1l[...], NN) + ratio * kept[0]
    odd = mm3(own_s, s1[...], s1l[...], NN) + ratio * kept[1]
    w_even, w_odd = kept[2], kept[3]
    terms = 2.0 * w_even * (even * even + odd * odd) + 4.0 * w_odd * (even * odd)
    energy = all_sum(terms)
    out[...] = jnp.broadcast_to(energy, out.shape)


def grid_second(me, step, got, tables, kept, waves):
    return pl.pallas_call(
        grid_second_kernel,
        out_shape=jax.ShapeDtypeStruct((SLOTS, TILES), F32),
        in_specs=[SMEM] + vmem(6),
        out_specs=pl.BlockSpec(memory_space=pltpu.VMEM),
        compiler_params=params(8),
        cost_estimate=cost(10**9, 5 * 10**6),
    )(me, step, got, *tables, kept, waves)


S_WIDTH = 512


def lookup_kernel(extra_row, got, z_high, z_low):
    lane = lax.broadcasted_iota(jnp.int32, (1, LANES), 1)
    blank = jnp.zeros((LANES - F_ROWS, TILES), F32)
    high, low = split(
        jnp.concatenate([x for g in range(GROUPS) for x in (got[g, 0:F_ROWS, :], blank)], 0)
    )
    order_rows = [got[g, extra_row : extra_row + 1, 0:LANES] for g in range(GROUPS)]
    for c in range(2):
        ours = (lane >= c * SLOTS) & (lane < (c + 1) * SLOTS)
        hits = jnp.concatenate([slot_hits(jnp.where(ours, row, -1.0)) for row in order_rows], 1)
        z_high[pl.ds(c * ORDERS, ORDERS), :] = dot(hits, high, NN).astype(BF)
        z_low[pl.ds(c * ORDERS, ORDERS), :] = dot(hits, low, NN).astype(BF)


def lookup(got, extra_row):
    shape = jax.ShapeDtypeStruct((2 * ORDERS, TILES), BF)
    return pl.pallas_call(
        lambda *refs: lookup_kernel(extra_row, *refs),
        out_shape=[shape, shape],
        in_specs=vmem(1),
        out_specs=vmem(2),
        compiler_params=params(10),
        cost_estimate=cost(10**9, 3 * 10**6),
    )(got)


def values_kernel(start, me, gate, high_r, low_r, tile_r, z_high, z_low, out):
    first = (me[0] + gate[0]) * (high_r.shape[1] // GROUPS) + start * S_WIDTH
    near_order = lax.broadcasted_iota(jnp.int32, (8, S_WIDTH), 0).astype(F32)

    def step(i, carry):
        at = pl.ds(pl.multiple_of(first + i * S_WIDTH, S_WIDTH), S_WIDTH)
        hits_here = tile_hits(tile_r[:, at], S_WIDTH)
        picked = dot(z_high[...], hits_here, NN) + dot(z_low[...], hits_here, NN)
        high, low = high_r[:, at], low_r[:, at]
        c, s = turn_trig(near_order, high, low)
        c8, s8 = turn_trig(8.0, high, low)
        c8 = jnp.broadcast_to(c8, c.shape)
        s8 = jnp.broadcast_to(s8, c.shape)
        total = None
        for b in range(ORDERS // 8):
            add = c * picked[8 * b : 8 * b + 8, :] + s * picked[ORDERS + 8 * b : ORDERS + 8 * b + 8, :]
            total = add if total is None else total + add
            c, s = c * c8 - s * s8, s * c8 + c * s8
        row = jnp.sum(total, axis=0, keepdims=True)
        for j in range(S_WIDTH // LANES):
            out[pl.ds(i * (S_WIDTH // LANES) + j, 1), :] = row[:, j * LANES : (j + 1) * LANES]
        return carry

    lax.fori_loop(0, out.shape[0] * LANES // S_WIDTH, step, 0, unroll=10)


def point_values(me, points, tables, start, rows, gate):
    high, low, tile = points
    return pl.pallas_call(
        lambda *refs: values_kernel(start, *refs),
        out_shape=jax.ShapeDtypeStruct((rows * S_WIDTH // LANES, LANES), F32),
        in_specs=[SMEM, SMEM] + vmem(5),
        out_specs=pl.BlockSpec(memory_space=pltpu.VMEM),
        compiler_params=params(10),
        cost_estimate=cost(8 * ORDERS * TILES * rows * S_WIDTH, 10**6),
    )(me, gate, high, low, tile, *tables)


def final_kernel(last, step, got, vector, next_vector, observed, fitted, coefficients):
    rows = fitted.shape[1]
    alpha, norm, prior_00 = step[0:1, 0:1], step[1:2, 0:1], step[2:3, 0:1]
    norm_1 = source_sum(got, EXTRA_SECOND + 1)
    prior_01 = source_sum(got, EXTRA_SECOND + 2)
    prior_11 = source_sum(got, EXTRA_SECOND + 3)
    energy = source_sum(last, 2 * rows)
    ratio = norm_1 / norm
    curvature = energy * (INV * INV) + prior_11 + 2.0 * ratio * prior_01 + ratio * ratio * prior_00
    beta = norm_1 / curvature
    on_first = alpha + beta * ratio
    coefficients[...] = on_first * vector[...] + beta * next_vector[...]
    on_first, beta = on_first * INV, beta * INV
    for g in range(GROUPS):
        fitted[g] = observed[g] - (on_first * last[g, 0:rows, :] + beta * last[g, rows : 2 * rows, :])


def final(last, step, got, vector, next_vector, observed):
    return pl.pallas_call(
        final_kernel,
        out_shape=[
            jax.ShapeDtypeStruct(observed.shape, F32),
            jax.ShapeDtypeStruct(vector.shape, F32),
        ],
        in_specs=vmem(6),
        out_specs=vmem(2),
        compiler_params=params(8),
        cost_estimate=cost(10**7, 3 * 10**6),
    )(last, step, got, vector, next_vector, observed)


def waves():
    k = np.arange(ORDERS)[:, None]
    q = np.arange(HALF)[None, :] * 2 + 1
    phase = 2 * np.pi * ((k * q) % (2 * GRID)) / (2 * GRID)
    out = []
    for f in (np.cos(phase), np.sin(phase)):
        high = f.astype(jnp.bfloat16)
        out += [high, (f - high.astype(np.float64)).astype(jnp.bfloat16)]
    return np.concatenate(out, 0)


def sectoral_values(orders, sines):
    single = (orders == 0.0).astype(F32)
    log_lead = 0.5 * (
        jnp.log(2.0 - single)
        + lax.lgamma(orders + 1.5)
        - lax.lgamma(orders * 0.0 + 1.5)
        - lax.lgamma(orders + 1.0)
    )
    return jnp.exp(log_lead + orders * jnp.log(sines))


def exchange(x, d):
    return lax.ppermute(x, "pts", [(i, i ^ d) for i in range(16)])


def gated(x, move, task):
    if task is None:
        return move(x), None
    x, gate = lax.optimization_barrier((x, jnp.zeros((1,), jnp.int32)))
    return lax.optimization_barrier((move(x), task(gate)))


def chips_total(x, tasks):
    (x, across, near, both), first = gated(
        x, lambda v: (v, exchange(v, 4), exchange(v, 2), exchange(v, 6)), tasks[0]
    )
    x = (x + across) + (near + both)
    (x, far), second = gated(x, lambda v: (v, exchange(v, 8)), tasks[1])
    return x + far, [first, second]


def halves_total(keep, give, tasks=(None, None)):
    x, made = chips_total(keep + exchange(give, 1), tasks)
    return (x, exchange(x, 1)), made


def swap(x):
    return lax.all_to_all(x, "coef", 0, 0)


def shards(colatitude, longitude, tile_of_point, order_of_slot, observations, obs_weight, prior):
    me = lax.axis_index("coef").astype(jnp.int32).reshape(1)
    place = lax.axis_index("pts").astype(jnp.int32)
    core = (place & 1).reshape(1)
    me, core, place, order_of_slot, longitude, tile_of_point = lax.optimization_barrier(
        (me, core, place * TILES, order_of_slot, longitude, tile_of_point)
    )
    local_tile = (tile_of_point - place).astype(F32)
    order = order_of_slot.astype(F32)
    orders = jnp.broadcast_to(order[:, None], (SLOTS, LANES))
    cosine = jnp.cos(colatitude)[None, :]
    sectoral = sectoral_values(order[:, None], jnp.sin(colatitude)[None, :])
    degree = np.arange(DEG_PAD, dtype=np.float64)
    scale = jnp.asarray((1.0 / (4 * degree * degree - 1)).astype(np.float32))
    wave = jnp.asarray(waves())

    turn = 2.0 * math.pi
    turn_high = 6.28125
    turn_low = turn - turn_high
    high = jnp.round(longitude * (4096.0 / turn)) * (1.0 / 4096.0)
    low = ((longitude - high * turn_high) - high * turn_low) * (1.0 / turn)
    far = high * ORDERS
    far = ((far - jnp.round(far)) + low * ORDERS) * turn
    weighted = obs_weight * observations
    points = [x[None] for x in (high, low, obs_weight, weighted, jnp.cos(far), jnp.sin(far), local_tile)]
    near = points[0], points[1], points[6]

    field, w_first, w_second = moments(points, orders)
    p_high, p_low = legendre_table(orders, cosine, sectoral, scale)
    prior_row = jnp.pad(prior, (0, DEG_PAD - DEGREES))[None, :]
    order_row = jnp.concatenate([order, order, jnp.full((LANES - 2 * SLOTS,), -1.0, F32)])[None]
    own_rows = high.shape[0] // (GROUPS * S_WIDTH)
    half = own_rows // 2

    halves, _ = halves_total(*unfold(core, field, p_high, p_low, False))
    sent, residual = fold_first(core, halves, p_high, p_low, prior_row, order_row, w_first, w_second)
    sent, me, core = lax.optimization_barrier((sent, me, core))
    got, me, core = lax.optimization_barrier((swap(sent), me, core))

    tables_0 = lookup(got, EXTRA_FIRST)
    back, kept = grid_first(me, got, tables_0, wave)
    held = (me, core, tables_0, kept, near)
    back, held = lax.optimization_barrier((back, held))
    seen, (me, core, tables_0, kept, near) = lax.optimization_barrier((swap(back), held))
    halves, values_0 = halves_total(
        *unfold(core, seen, p_high, p_low, True),
        [
            lambda gate: point_values(me, near, tables_0, 0, half, gate),
            lambda gate: point_values(me, near, tables_0, half, own_rows - half, gate),
        ],
    )
    sent_1, residual_1, step = fold_second(core, halves, residual, got, p_high, p_low, prior_row, order_row)
    held = (me, values_0, kept, near, residual, residual_1, step)
    sent_1, held = lax.optimization_barrier((sent_1, held))
    got_1, held = lax.optimization_barrier((swap(sent_1), held))
    me, values_0, kept, near, residual, residual_1, step = held
    tables_1 = lookup(got_1, EXTRA_SECOND)
    part = grid_second(me, step, got_1, tables_1, kept, wave)
    energy_1, values_1 = chips_total(
        part + exchange(part, 1),
        [
            lambda gate: point_values(me, near, tables_1, 0, half, gate),
            lambda gate: point_values(me, near, tables_1, half, own_rows - half, gate),
        ],
    )
    payload = jnp.concatenate(
        values_0 + values_1 + [energy_1[0:8, 0:LANES]], 0
    )
    last = swap(jnp.broadcast_to(payload[None], (GROUPS,) + payload.shape))
    residual_out, vector = final(
        last, step, got_1, residual, residual_1, observations.reshape(GROUPS, -1, LANES)
    )
    coefficients = vector.reshape(2, SLOTS, DEG_PAD)[:, :, :DEGREES].transpose(2, 0, 1)
    return coefficients, residual_out.reshape(-1)


def solution(mesh):
    placed = (P("pts"), P("pts"), P("pts"), P("coef"), P("pts"), P("pts"), P())
    return jax.shard_map(
        shards,
        mesh=mesh,
        in_specs=placed,
        out_specs=(P(None, None, "coef"), P("pts")),
        check_vma=False,
    )
```

```python
import math
import numpy as np
import jax
import jax.numpy as jnp
from jax import lax
from jax.experimental import pallas as pl
from jax.experimental.pallas import tpu as pltpu
from jax.sharding import PartitionSpec as P

DEGREES = 301
DEG_PAD = 304
SLOTS = 40
TILES = 256
GROUPS = 8
OWN_TILES = TILES // GROUPS
ORDERS = 320
GRID = 1280
HALF = GRID // 2
LANES = 128
INV = 1.0 / DEGREES
BF = jnp.bfloat16
F32 = jnp.float32
ROUNDER = 12582912.0

NN = (((1,), (0,)), ((), ()))
NT = (((1,), (1,)), ((), ()))


def fit_even(f, terms):
    r = 0.502 * np.cos((np.arange(400) + 0.5) * np.pi / 800)
    a = np.stack([r ** (2 * k) for k in range(terms)], 1)
    return [float(v) for v in np.linalg.lstsq(a, f(r), rcond=None)[0]]


SIN_TERMS = fit_even(lambda r: np.sin(np.pi * r) / r, 5)
COS_TERMS = fit_even(lambda r: np.cos(np.pi * r), 5)


def horner(x, terms):
    total = terms[-1] * x + terms[-2]
    for term in terms[-3::-1]:
        total = total * x + term
    return total


def turn_trig(order, high, low):
    whole = order * high
    near = (whole + ROUNDER) - ROUNDER
    part = (whole - near) + order * low
    square = part * part
    s = horner(square, SIN_TERMS) * part
    c = horner(square, COS_TERMS)
    twice = s + s
    return 1.0 - twice * s, twice * c


def split(x):
    high = x.astype(BF)
    return high, (x - high.astype(F32)).astype(BF)


def dot(a, b, dims):
    return lax.dot_general(a, b, dims, preferred_element_type=F32)


def mm3(x, b_high, b_low, dims):
    rows = x.shape[0]
    high, low = split(x)
    both = dot(jnp.concatenate([high, low], 0), b_high, dims)
    return both[:rows] + both[rows:] + dot(high, b_low, dims)


def vmem(n):
    return [pl.BlockSpec(memory_space=pltpu.VMEM)] * n


SMEM = pl.BlockSpec(memory_space=pltpu.SMEM)


def params(mib):
    return pltpu.CompilerParams(vmem_limit_bytes=mib * 2**20)


def cost(flops, bytes_accessed):
    return pl.CostEstimate(flops=flops, bytes_accessed=bytes_accessed, transcendentals=0)


def tile_hits(tile_row, width):
    ids = lax.broadcasted_iota(jnp.int32, (TILES, width), 0).astype(F32)
    return jnp.where(ids == tile_row, 1.0, 0.0).astype(BF)


WIDTH = 2048
UNROLL = 4


def moments_kernel(high_r, low_r, weight_r, value_r, c_far_r, s_far_r, tile_r, orders, field, w_first, w_second, total):
    total[...] = jnp.zeros_like(total)
    order = orders[...]

    def make(first):
        parts = []
        for j in range(WIDTH // LANES):
            at = pl.ds(pl.multiple_of(first + j * LANES, LANES), LANES)
            c, s = turn_trig(order, high_r[:, at], low_r[:, at])
            weight, value = weight_r[:, at], value_r[:, at]
            c_far, s_far = c_far_r[:, at], s_far_r[:, at]
            wc, ws = weight * c, weight * s
            rows = jnp.concatenate(
                [value * c, value * s, wc, ws, wc * c_far - ws * s_far, ws * c_far + wc * s_far], 0
            )
            parts.append(split(rows) + (tile_hits(tile_r[:, at], LANES),))
        high, low, hits = [jnp.concatenate(x, 1) for x in zip(*parts)]
        return jnp.concatenate([high, low], 0), hits

    def step(i, carry):
        add = None
        for part in range(UNROLL):
            rows, hits = make((i * UNROLL + part) * WIDTH)
            got = dot(rows, hits, NT)
            add = got if add is None else add + got
        total[...] += add
        return carry

    lax.fori_loop(0, high_r.shape[1] // (WIDTH * UNROLL), step, 0)
    whole = total[0 : 6 * SLOTS] + total[6 * SLOTS : 12 * SLOTS]
    field[...] = whole[0 : 2 * SLOTS]
    blank = jnp.zeros((LANES - 2 * SLOTS, TILES), F32)
    w_first[...] = jnp.concatenate([whole[2 * SLOTS : 4 * SLOTS], blank], 0).T
    w_second[...] = jnp.concatenate([whole[4 * SLOTS : 6 * SLOTS], blank], 0).T


def moments(points, orders):
    n = points[0].shape[1]
    return pl.pallas_call(
        moments_kernel,
        out_shape=[
            jax.ShapeDtypeStruct((2 * SLOTS, TILES), F32),
            jax.ShapeDtypeStruct((TILES, LANES), F32),
            jax.ShapeDtypeStruct((TILES, LANES), F32),
        ],
        in_specs=vmem(8),
        out_specs=vmem(3),
        scratch_shapes=[pltpu.VMEM((12 * SLOTS, TILES), F32)],
        compiler_params=params(12),
        cost_estimate=cost(2 * 12 * SLOTS * TILES * n, 32 * n),
    )(*points, orders)


def table_kernel(orders, cosine, sectoral, scale, p_high, p_low, left, right):
    order = jnp.broadcast_to(orders[:, 0:1], (SLOTS, TILES))
    order_sq = orders[...] * orders[...]
    cos_row = jnp.broadcast_to(cosine[...], (SLOTS, TILES))
    start = sectoral[...]

    def put(n, value):
        for b in range(SLOTS // 8):
            at = pl.ds(b * 8 * DEG_PAD + n, 8, stride=DEG_PAD)
            left[at, :] = value[8 * b : 8 * b + 8, 0:LANES]
            right[at, :] = value[8 * b : 8 * b + 8, LANES:TILES]

    def step(n, carried):
        recent, earlier, back = carried
        degree = n.astype(F32)
        ratio = jnp.maximum((degree * degree - order_sq) * scale[n], 1e-20)
        up = lax.rsqrt(ratio)
        this_back = ratio * up
        up2 = jnp.concatenate([up, up], 1)
        back2 = jnp.concatenate([back, back], 1)
        grown = up2 * (cos_row * recent - back2 * earlier)
        value = jnp.where(order > degree, 0.0, jnp.where(order == degree, start, grown))
        put(n, value)
        return value, recent, this_back

    empty = jnp.zeros((SLOTS, TILES), F32)
    unset = start * 0.0
    lax.fori_loop(0, DEG_PAD, step, (unset, unset, order_sq * 0.0), unroll=8)
    for n in range(DEGREES, DEG_PAD):
        put(n, empty)

    def pack(slot, carry):
        at = pl.ds(pl.multiple_of(slot * DEG_PAD, 8), DEG_PAD)
        high, low = split(jnp.concatenate([left[at, :], right[at, :]], 1))
        p_high[slot] = high
        p_low[slot] = low
        return carry

    lax.fori_loop(0, SLOTS, pack, 0, unroll=4)


def legendre_table(orders, cosine, sectoral, scale):
    shape = jax.ShapeDtypeStruct((SLOTS, DEG_PAD, TILES), BF)
    return pl.pallas_call(
        table_kernel,
        out_shape=[shape, shape],
        in_specs=vmem(3) + [SMEM],
        out_specs=vmem(2),
        scratch_shapes=[pltpu.VMEM((SLOTS * DEG_PAD, LANES), F32)] * 2,
        compiler_params=params(30),
        cost_estimate=cost(20 * SLOTS * DEG_PAD * TILES, 4 * SLOTS * DEG_PAD * TILES),
    )(orders, cosine, sectoral, scale)


def slot_group(vector, at, high_of, low_of, width, dims):
    row = lax.broadcasted_iota(jnp.int32, (16, width), 0)
    rows = jnp.concatenate([vector[pl.ds(at, 8), :], vector[pl.ds(at + SLOTS, 8), :]], 0)
    high, low = split(rows)
    both = jnp.concatenate([high, low], 0)
    out = jnp.zeros((16, width), F32)
    for i in range(8):
        first = dot(both, high_of(at + i), dims)
        total = first[0:16] + first[16:32] + dot(high, low_of(at + i), dims)
        out = jnp.where((row == i) | (row == i + 8), total, out)
    return out


def by_slot(vector, p_high, p_low, width, dims, put, ready=None):
    def group(g, carry):
        at = pl.multiple_of(g * 8, 8)
        if ready is not None:
            ready(g)
        put(at, slot_group(vector, at, lambda i: p_high[i], lambda i: p_low[i], width, dims))
        return carry

    lax.fori_loop(0, SLOTS // 8, group, 0, unroll=True)


F_ROWS = 2 * SLOTS
EXTRA_FIRST = F_ROWS + OWN_TILES
EXTRA_SECOND = F_ROWS


def all_sum(x):
    return jnp.sum(jnp.sum(x, axis=1, keepdims=True), axis=0, keepdims=True)


def extra_rows(order_row, sums):
    rows = [order_row] + [jnp.broadcast_to(x, (1, LANES)) for x in sums]
    rows = jnp.concatenate(rows + [jnp.zeros((8 - len(rows), LANES), F32)], 0)
    return jnp.concatenate([rows, rows], 1)


def source_sum(got, row):
    total = got[0, row : row + 1, 0:1]
    for g in range(1, GROUPS):
        total = total + got[g, row : row + 1, 0:1]
    return total


def fold_into(vector, p_high, p_low, rows):
    def put(at, value):
        rows[pl.ds(at, 8), :] = value[0:8]
        rows[pl.ds(at + SLOTS, 8), :] = value[8:16]

    by_slot(vector, p_high, p_low, TILES, NN, put)
    return rows[...]


def join(core, mine, other):
    even = core[0] == 0
    mine, other = mine[...], other[...]
    return jnp.concatenate([jnp.where(even, mine, other), jnp.where(even, other, mine)], 0)


def fold_first_kernel(core, mine, other, p_high, p_low, prior, order_row, w_first, w_second, sent, vector, rows):
    v = join(core, mine, other)
    vector[...] = v
    folded = fold_into(vector, p_high, p_low, rows)
    extra = extra_rows(order_row[...], [all_sum(v * v), all_sum(prior[...] * v * v)])
    t = OWN_TILES
    for g in range(GROUPS):
        sent[g, 0:F_ROWS, :] = folded
        sent[g, F_ROWS:EXTRA_FIRST, 0:LANES] = w_first[g * t : (g + 1) * t, :]
        sent[g, F_ROWS:EXTRA_FIRST, LANES:TILES] = w_second[g * t : (g + 1) * t, :]
        sent[g, EXTRA_FIRST : EXTRA_FIRST + 8, :] = extra


def fold_first(core, halves, p_high, p_low, prior, order_row, w_first, w_second):
    return pl.pallas_call(
        fold_first_kernel,
        out_shape=[
            jax.ShapeDtypeStruct((GROUPS, EXTRA_FIRST + 8, TILES), F32),
            jax.ShapeDtypeStruct((2 * SLOTS, DEG_PAD), F32),
        ],
        in_specs=[SMEM] + vmem(8),
        out_specs=vmem(2),
        scratch_shapes=[pltpu.VMEM((2 * SLOTS, TILES), F32)],
        compiler_params=params(20),
        cost_estimate=cost(64 * SLOTS * DEG_PAD * TILES, 4 * SLOTS * DEG_PAD * TILES),
    )(core, *halves, p_high, p_low, prior, order_row, w_first, w_second)


def fold_second_kernel(core, mine, other, vector, got, p_high, p_low, prior, order_row, sent, next_vector, step, rows):
    v = vector[...]
    applied = join(core, mine, other)
    lane = lax.broadcasted_iota(jnp.int32, v.shape, 1)
    norm = source_sum(got, EXTRA_FIRST + 1)
    weighed = source_sum(got, EXTRA_FIRST + 2)
    alpha = norm / (applied[0:1, DEGREES : DEGREES + 1] * (INV * INV) + weighed)
    r = v - alpha * jnp.where(lane < DEGREES, applied + prior[...] * v, 0.0)
    next_vector[...] = r
    step[...] = jnp.concatenate(
        [jnp.broadcast_to(x, (1, LANES)) for x in (alpha, norm, weighed)] + [jnp.zeros((5, LANES), F32)], 0
    )
    folded = fold_into(next_vector, p_high, p_low, rows)
    extra = extra_rows(
        order_row[...], [all_sum(r * r), all_sum(prior[...] * v * r), all_sum(prior[...] * r * r)]
    )
    for g in range(GROUPS):
        sent[g, 0:F_ROWS, :] = folded
        sent[g, EXTRA_SECOND : EXTRA_SECOND + 8, :] = extra


def fold_second(core, halves, vector, got, p_high, p_low, prior, order_row):
    return pl.pallas_call(
        fold_second_kernel,
        out_shape=[
            jax.ShapeDtypeStruct((GROUPS, EXTRA_SECOND + 8, TILES), F32),
            jax.ShapeDtypeStruct((2 * SLOTS, DEG_PAD), F32),
            jax.ShapeDtypeStruct((8, LANES), F32),
        ],
        in_specs=[SMEM] + vmem(8),
        out_specs=vmem(3),
        scratch_shapes=[pltpu.VMEM((2 * SLOTS, TILES), F32)],
        compiler_params=params(20),
        cost_estimate=cost(64 * SLOTS * DEG_PAD * TILES, 4 * SLOTS * DEG_PAD * TILES),
    )(core, *halves, vector, got, p_high, p_low, prior, order_row)


def put_halves(core, keep, give, at, first, second):
    even = core[0] == 0
    keep[pl.ds(at, 8), :] = jnp.where(even, first, second)
    give[pl.ds(at, 8), :] = jnp.where(even, second, first)


def unfold_first_kernel(core, field, p_high, p_low, keep, give):
    def put(at, value):
        put_halves(core, keep, give, at, value[0:8] * INV, value[8:16] * INV)

    by_slot(field, p_high, p_low, DEG_PAD, NT, put)


def unfold_second_kernel(core, seen, p_high, p_low, keep, give, rows):
    t = OWN_TILES
    rows[...] = jnp.concatenate([seen[g, 0:t, :] for g in range(GROUPS)], 0).T
    energy = source_sum(seen, t)
    lane = lax.broadcasted_iota(jnp.int32, (8, DEG_PAD), 1)

    def put(at, value):
        first = jnp.where(lane == DEGREES, energy, value[0:8] * (INV * INV))
        put_halves(core, keep, give, at, first, value[8:16] * (INV * INV))

    by_slot(rows, p_high, p_low, DEG_PAD, NT, put)


def unfold(core, field, p_high, p_low, second):
    half = jax.ShapeDtypeStruct((SLOTS, DEG_PAD), F32)
    return pl.pallas_call(
        unfold_second_kernel if second else unfold_first_kernel,
        out_shape=[half, half],
        in_specs=[SMEM] + vmem(3),
        out_specs=vmem(2),
        scratch_shapes=[pltpu.VMEM((LANES, TILES), F32)] if second else [],
        compiler_params=params(20),
        cost_estimate=cost(64 * SLOTS * DEG_PAD * TILES, 4 * SLOTS * DEG_PAD * TILES),
    )(core, field, p_high, p_low)


def slot_hits(order_row):
    wanted = lax.broadcasted_iota(jnp.int32, (ORDERS, LANES), 0).astype(F32)
    return jnp.where(wanted == order_row, 1.0, 0.0).astype(BF)


def two_halves(x):
    lane = lax.broadcasted_iota(jnp.int32, x.shape, 1)
    return jnp.where(lane < SLOTS, x, 0.0), jnp.where((lane >= SLOTS) & (lane < 2 * SLOTS), x, 0.0)


def to_natural(pieces, hits):
    total = None
    for per_source, hit in zip(pieces, hits):
        rows = [half for x in per_source for half in two_halves(x)]
        high, low = split(jnp.concatenate(rows, 0))
        got = dot(jnp.concatenate([high, low], 0), hit, NT)
        total = got if total is None else total + got
    n = total.shape[0] // 2
    return total[:n] + total[n:]


def own_tiles(me, z_high, z_low):
    shape = (OWN_TILES, TILES)
    wanted = lax.broadcasted_iota(jnp.int32, shape, 0) + me[0] * OWN_TILES
    pick = jnp.where(lax.broadcasted_iota(jnp.int32, shape, 1) == wanted, 1.0, 0.0).astype(BF)
    return [
        dot(pick, z_high[pl.ds(c * ORDERS, ORDERS), :], NT) + dot(pick, z_low[pl.ds(c * ORDERS, ORDERS), :], NT)
        for c in range(2)
    ]


def wave_parts(wave):
    return [wave.at[pl.ds(i * ORDERS, ORDERS), :] for i in range(4)]


def grid_first_kernel(me, got, z_high, z_low, wave, back, kept):
    c1, c1l, s1, s1l = wave_parts(wave)
    t = OWN_TILES
    hits = [slot_hits(got[g, EXTRA_FIRST : EXTRA_FIRST + 1, 0:LANES]) for g in range(GROUPS)]
    nat = to_natural(
        [
            [got[g, F_ROWS:EXTRA_FIRST, 0:LANES], got[g, F_ROWS:EXTRA_FIRST, LANES:TILES]]
            for g in range(GROUPS)
        ],
        hits,
    )
    own_c, own_s = own_tiles(me, z_high, z_low)
    k = lax.broadcasted_iota(jnp.int32, (1, ORDERS), 1)
    k_first = jnp.where(k == 0, 1.0 / GRID, 2.0 / GRID)
    k_second = jnp.where(k + ORDERS <= 2 * (DEGREES - 1), 2.0 / GRID, 0.0)
    near_c, near_s = nat[0:t] * k_first, nat[t : 2 * t] * k_first
    far_c, far_s = nat[2 * t : 3 * t] * k_second, nat[3 * t :] * k_second
    by_c = mm3(jnp.concatenate([own_c, near_c, far_c, far_s], 0), c1[...], c1l[...], NN)
    by_s = mm3(jnp.concatenate([own_s, near_s, far_c, far_s], 0), s1[...], s1l[...], NN)
    q = lax.broadcasted_iota(jnp.int32, (1, HALF), 1) % 4
    root = math.sqrt(0.5)
    turn_c = jnp.where((q == 0) | (q == 3), root, -root)
    turn_s = jnp.where(q < 2, root, -root)
    even, odd = by_c[:t], by_s[:t]
    w_even = by_c[t : 2 * t] + turn_c * by_c[2 * t : 3 * t] - turn_s * by_s[2 * t : 3 * t]
    w_odd = by_s[t : 2 * t] + turn_c * by_s[3 * t :] + turn_s * by_c[3 * t :]
    h_even = 2.0 * (w_even * even + w_odd * odd)
    h_odd = 2.0 * (w_even * odd + w_odd * even)
    energy = all_sum(h_even * even + h_odd * odd)
    kept[0] = even
    kept[1] = odd
    kept[2] = w_even
    kept[3] = w_odd
    hc = mm3(h_even, c1[...], c1l[...], NT)
    hs = mm3(h_odd, s1[...], s1l[...], NT)
    c_high, c_low = split(hc)
    s_high, s_low = split(hs)
    stack = jnp.concatenate([c_high, c_low, s_high, s_low], 0)
    lane = lax.broadcasted_iota(jnp.int32, (t, LANES), 1)
    for g in range(GROUPS):
        slots = dot(stack, hits[g], NN)
        back[g, 0:t, :] = jnp.where(
            lane < SLOTS, slots[0:t] + slots[t : 2 * t], slots[2 * t : 3 * t] + slots[3 * t :]
        )
        back[g, t : t + 8, :] = jnp.broadcast_to(energy, (8, LANES))


def grid_first(me, got, tables, waves):
    return pl.pallas_call(
        grid_first_kernel,
        out_shape=[
            jax.ShapeDtypeStruct((GROUPS, OWN_TILES + 8, LANES), F32),
            jax.ShapeDtypeStruct((4, OWN_TILES, HALF), F32),
        ],
        in_specs=[SMEM] + vmem(4),
        out_specs=vmem(2),
        compiler_params=params(8),
        cost_estimate=cost(10**9, 5 * 10**6),
    )(me, got, *tables, waves)


def grid_second_kernel(me, step, got, z_high, z_low, kept, wave, out):
    c1, c1l, s1, s1l = wave_parts(wave)
    own_c, own_s = own_tiles(me, z_high, z_low)
    ratio = source_sum(got, EXTRA_SECOND + 1) / step[1:2, 0:1]
    even = mm3(own_c, c1[...], c1l[...], NN) + ratio * kept[0]
    odd = mm3(own_s, s1[...], s1l[...], NN) + ratio * kept[1]
    w_even, w_odd = kept[2], kept[3]
    terms = 2.0 * w_even * (even * even + odd * odd) + 4.0 * w_odd * (even * odd)
    energy = all_sum(terms)
    out[...] = jnp.broadcast_to(energy, out.shape)


def grid_second(me, step, got, tables, kept, waves):
    return pl.pallas_call(
        grid_second_kernel,
        out_shape=jax.ShapeDtypeStruct((SLOTS, TILES), F32),
        in_specs=[SMEM] + vmem(6),
        out_specs=pl.BlockSpec(memory_space=pltpu.VMEM),
        compiler_params=params(8),
        cost_estimate=cost(10**9, 5 * 10**6),
    )(me, step, got, *tables, kept, waves)


S_WIDTH = 512


def lookup_kernel(extra_row, got, z_high, z_low):
    lane = lax.broadcasted_iota(jnp.int32, (1, LANES), 1)
    blank = jnp.zeros((LANES - F_ROWS, TILES), F32)
    high, low = split(
        jnp.concatenate([x for g in range(GROUPS) for x in (got[g, 0:F_ROWS, :], blank)], 0)
    )
    order_rows = [got[g, extra_row : extra_row + 1, 0:LANES] for g in range(GROUPS)]
    for c in range(2):
        ours = (lane >= c * SLOTS) & (lane < (c + 1) * SLOTS)
        hits = jnp.concatenate([slot_hits(jnp.where(ours, row, -1.0)) for row in order_rows], 1)
        z_high[pl.ds(c * ORDERS, ORDERS), :] = dot(hits, high, NN).astype(BF)
        z_low[pl.ds(c * ORDERS, ORDERS), :] = dot(hits, low, NN).astype(BF)


def lookup(got, extra_row):
    shape = jax.ShapeDtypeStruct((2 * ORDERS, TILES), BF)
    return pl.pallas_call(
        lambda *refs: lookup_kernel(extra_row, *refs),
        out_shape=[shape, shape],
        in_specs=vmem(1),
        out_specs=vmem(2),
        compiler_params=params(10),
        cost_estimate=cost(10**9, 3 * 10**6),
    )(got)


def values_kernel(start, me, gate, high_r, low_r, tile_r, z_high, z_low, out):
    first = (me[0] + gate[0]) * (high_r.shape[1] // GROUPS) + start * S_WIDTH
    near_order = lax.broadcasted_iota(jnp.int32, (8, S_WIDTH), 0).astype(F32)

    def step(i, carry):
        at = pl.ds(pl.multiple_of(first + i * S_WIDTH, S_WIDTH), S_WIDTH)
        hits_here = tile_hits(tile_r[:, at], S_WIDTH)
        picked = dot(z_high[...], hits_here, NN) + dot(z_low[...], hits_here, NN)
        high, low = high_r[:, at], low_r[:, at]
        c, s = turn_trig(near_order, high, low)
        c8, s8 = turn_trig(8.0, high, low)
        c8 = jnp.broadcast_to(c8, c.shape)
        s8 = jnp.broadcast_to(s8, c.shape)
        total = None
        for b in range(ORDERS // 8):
            add = c * picked[8 * b : 8 * b + 8, :] + s * picked[ORDERS + 8 * b : ORDERS + 8 * b + 8, :]
            total = add if total is None else total + add
            c, s = c * c8 - s * s8, s * c8 + c * s8
        row = jnp.sum(total, axis=0, keepdims=True)
        for j in range(S_WIDTH // LANES):
            out[pl.ds(i * (S_WIDTH // LANES) + j, 1), :] = row[:, j * LANES : (j + 1) * LANES]
        return carry

    lax.fori_loop(0, out.shape[0] * LANES // S_WIDTH, step, 0, unroll=10)


def point_values(me, points, tables, start, rows, gate):
    high, low, tile = points
    return pl.pallas_call(
        lambda *refs: values_kernel(start, *refs),
        out_shape=jax.ShapeDtypeStruct((rows * S_WIDTH // LANES, LANES), F32),
        in_specs=[SMEM, SMEM] + vmem(5),
        out_specs=pl.BlockSpec(memory_space=pltpu.VMEM),
        compiler_params=params(10),
        cost_estimate=cost(8 * ORDERS * TILES * rows * S_WIDTH, 10**6),
    )(me, gate, high, low, tile, *tables)


def final_kernel(last, step, got, vector, next_vector, observed, fitted, coefficients):
    rows = fitted.shape[1]
    alpha, norm, prior_00 = step[0:1, 0:1], step[1:2, 0:1], step[2:3, 0:1]
    norm_1 = source_sum(got, EXTRA_SECOND + 1)
    prior_01 = source_sum(got, EXTRA_SECOND + 2)
    prior_11 = source_sum(got, EXTRA_SECOND + 3)
    energy = source_sum(last, 2 * rows)
    ratio = norm_1 / norm
    curvature = energy * (INV * INV) + prior_11 + 2.0 * ratio * prior_01 + ratio * ratio * prior_00
    beta = norm_1 / curvature
    on_first = alpha + beta * ratio
    coefficients[...] = on_first * vector[...] + beta * next_vector[...]
    on_first, beta = on_first * INV, beta * INV
    for g in range(GROUPS):
        fitted[g] = observed[g] - (on_first * last[g, 0:rows, :] + beta * last[g, rows : 2 * rows, :])


def final(last, step, got, vector, next_vector, observed):
    return pl.pallas_call(
        final_kernel,
        out_shape=[
            jax.ShapeDtypeStruct(observed.shape, F32),
            jax.ShapeDtypeStruct(vector.shape, F32),
        ],
        in_specs=vmem(6),
        out_specs=vmem(2),
        compiler_params=params(8),
        cost_estimate=cost(10**7, 3 * 10**6),
    )(last, step, got, vector, next_vector, observed)


def waves():
    k = np.arange(ORDERS)[:, None]
    q = np.arange(HALF)[None, :] * 2 + 1
    phase = 2 * np.pi * ((k * q) % (2 * GRID)) / (2 * GRID)
    out = []
    for f in (np.cos(phase), np.sin(phase)):
        high = f.astype(jnp.bfloat16)
        out += [high, (f - high.astype(np.float64)).astype(jnp.bfloat16)]
    return np.concatenate(out, 0)


def sectoral_values(orders, sines):
    single = (orders == 0.0).astype(F32)
    log_lead = 0.5 * (
        jnp.log(2.0 - single)
        + lax.lgamma(orders + 1.5)
        - lax.lgamma(orders * 0.0 + 1.5)
        - lax.lgamma(orders + 1.0)
    )
    return jnp.exp(log_lead + orders * jnp.log(sines))


def exchange(x, d):
    return lax.ppermute(x, "pts", [(i, i ^ d) for i in range(16)])


def gated(x, move, task):
    if task is None:
        return move(x), None
    x, gate = lax.optimization_barrier((x, jnp.zeros((1,), jnp.int32)))
    return lax.optimization_barrier((move(x), task(gate)))


def chips_near(x, task):
    (x, across, near, both), made = gated(x, lambda v: (v, exchange(v, 4), exchange(v, 2), exchange(v, 6)), task)
    return (x + across) + (near + both), (made, None)


def chips_total(x, tasks):
    x, (first, _) = chips_near(x, tasks[0])
    (x, far), second = gated(x, lambda v: (v, exchange(v, 8)), tasks[1])
    return x + far, [first, second]


def halves_total(keep, give, tasks=(None, None)):
    x, made = chips_total(keep + exchange(give, 1), tasks)
    return (x, exchange(x, 1)), made


def swap(x):
    return lax.all_to_all(x, "coef", 0, 0)


def shards(colatitude, longitude, tile_of_point, order_of_slot, observations, obs_weight, prior):
    me = lax.axis_index("coef").astype(jnp.int32).reshape(1)
    place = lax.axis_index("pts").astype(jnp.int32)
    core = (place & 1).reshape(1)
    me, core, place, order_of_slot, longitude, tile_of_point = lax.optimization_barrier(
        (me, core, place * TILES, order_of_slot, longitude, tile_of_point)
    )
    local_tile = (tile_of_point - place).astype(F32)
    order = order_of_slot.astype(F32)
    orders = jnp.broadcast_to(order[:, None], (SLOTS, LANES))
    cosine = jnp.cos(colatitude)[None, :]
    sectoral = sectoral_values(order[:, None], jnp.sin(colatitude)[None, :])
    degree = np.arange(DEG_PAD, dtype=np.float64)
    scale = jnp.asarray((1.0 / (4 * degree * degree - 1)).astype(np.float32))
    wave = jnp.asarray(waves())

    turn = 2.0 * math.pi
    turn_high = 6.28125
    turn_low = turn - turn_high
    high = jnp.round(longitude * (4096.0 / turn)) * (1.0 / 4096.0)
    low = ((longitude - high * turn_high) - high * turn_low) * (1.0 / turn)
    far = high * ORDERS
    far = ((far - jnp.round(far)) + low * ORDERS) * turn
    weighted = obs_weight * observations
    points = [x[None] for x in (high, low, obs_weight, weighted, jnp.cos(far), jnp.sin(far), local_tile)]
    near = points[0], points[1], points[6]

    field, w_first, w_second = moments(points, orders)
    p_high, p_low = legendre_table(orders, cosine, sectoral, scale)
    prior_row = jnp.pad(prior, (0, DEG_PAD - DEGREES))[None, :]
    order_row = jnp.concatenate([order, order, jnp.full((LANES - 2 * SLOTS,), -1.0, F32)])[None]
    own_rows = high.shape[0] // (GROUPS * S_WIDTH)
    half = own_rows // 2

    halves, _ = halves_total(*unfold(core, field, p_high, p_low, False))
    sent, residual = fold_first(core, halves, p_high, p_low, prior_row, order_row, w_first, w_second)
    sent, me, core = lax.optimization_barrier((sent, me, core))
    got, me, core = lax.optimization_barrier((swap(sent), me, core))

    tables_0 = lookup(got, EXTRA_FIRST)
    back, kept = grid_first(me, got, tables_0, wave)
    held = (me, core, tables_0, kept, near)
    back, held = lax.optimization_barrier((back, held))
    seen, (me, core, tables_0, kept, near) = lax.optimization_barrier((swap(back), held))
    halves, values_0 = halves_total(
        *unfold(core, seen, p_high, p_low, True),
        [
            lambda gate: point_values(me, near, tables_0, 0, half, gate),
            lambda gate: point_values(me, near, tables_0, half, own_rows - half, gate),
        ],
    )
    sent_1, residual_1, step = fold_second(core, halves, residual, got, p_high, p_low, prior_row, order_row)
    held = (me, values_0, kept, near, residual, residual_1, step)
    sent_1, held = lax.optimization_barrier((sent_1, held))
    got_1, held = lax.optimization_barrier((swap(sent_1), held))
    me, values_0, kept, near, residual, residual_1, step = held
    tables_1 = lookup(got_1, EXTRA_SECOND)
    part = grid_second(me, step, got_1, tables_1, kept, wave)
    part = part + exchange(part, 1)
    (part, far), first = gated(
        part, lambda v: (v, exchange(v, 8)), lambda gate: point_values(me, near, tables_1, 0, half, gate)
    )
    energy_1, (second, _) = chips_near(
        part + far,
        lambda gate: point_values(me, near, tables_1, half, own_rows - half, gate),
    )
    values_1 = [first, second]
    payload = jnp.concatenate(
        values_0 + values_1 + [energy_1[0:8, 0:LANES]], 0
    )
    last = swap(jnp.broadcast_to(payload[None], (GROUPS,) + payload.shape))
    residual_out, vector = final(
        last, step, got_1, residual, residual_1, observations.reshape(GROUPS, -1, LANES)
    )
    coefficients = vector.reshape(2, SLOTS, DEG_PAD)[:, :, :DEGREES].transpose(2, 0, 1)
    return coefficients, residual_out.reshape(-1)


def solution(mesh):
    placed = (P("pts"), P("pts"), P("pts"), P("coef"), P("pts"), P("pts"), P())
    return jax.shard_map(
        shards,
        mesh=mesh,
        in_specs=placed,
        out_specs=(P(None, None, "coef"), P("pts")),
        check_vma=False,
    )
```
